32 devices in a mesh: grp: 2 (over x), seq: 16 (over z, y, core).
Axes of the slice: x: 2, y: 2, z: 4, core: 2. Of those that a mesh axis runs over, the one named last changes fastest.
Arguments:
- queries: bfloat16 [24576, 1024], P(('grp', 'seq')), parts along dimension 0, may hold values from -16 to 16
- key_states: bfloat16 [24576, 1024], P(('grp', 'seq')), parts along dimension 0, may hold values from -8 to 8
- values: bfloat16 [24576, 1024], P(('grp', 'seq')), parts along dimension 0, may hold values from -6 to 6
- grad_out: bfloat16 [24576, 1024], P(('grp', 'seq')), parts along dimension 0, may hold values from -6 to 6
- tile_pairs: int32 [192, 5], P('grp'), parts along dimension 0, may hold values from 0 to 95, as said below
- counts: int32 [192], P('grp'), parts along dimension 0, may hold values from 1 to 5
Outputs:
- grad_queries: bfloat16 [24576, 1024], P(('grp', 'seq')), parts along dimension 0
- grad_keys: bfloat16 [24576, 1024], P(('grp', 'seq')), parts along dimension 0
- grad_values: bfloat16 [24576, 1024], P(('grp', 'seq')), parts along dimension 0
The draws below stay inside these ranges and needn't reach their ends.
There are 2 independent parts, one for each index of `grp`. The reference program is written for one: setup_inputs(seed, part) draws one part's arguments, and reference() takes and returns one part's arrays. A program takes and returns all parts, laid end to end along the dimension named above; each array names one. Nothing has to cross between parts.
Inputs may be any that keep to these rules, and one draw needn't show every extreme that they name: `tile_pairs`: slot 0 of query tile t holds t itself; the first counts[t] slots hold distinct tiles within 2 tiles of t; the remaining slots hold tiles within that reach and are not attended.
All inputs are finite; a program needn't handle non-finite values.
Results may differ from the reference program's by a relative error of at most 0.0066.
Values may be sent and summed in bfloat16 or wider, within the bound.
No kernel may reach another device: no remote copies, remote signals or barrier semaphores. Data moves between devices by JAX's collectives and lax.ppermute only.
A program may use at most 128 MiB of HBM per device.

```python
import math
import jax
import jax.numpy as jnp
from jax import lax

HEAD_COUNT = 16
MODEL_WIDTH = 1024
TILE_REACH = 2
KEY_SLOTS = 5
SEQ_TOKENS = 12288
TILE_COUNT = 96
TILES_DEV = 6


def draw_queries(key, part):
    key = jax.random.fold_in(key, 11)
    scale_key, value_key = jax.random.split(key)
    row_scale = jnp.exp(jax.random.uniform(scale_key, (SEQ_TOKENS, 1), jnp.float32, math.log(0.4), math.log(4.0)))
    sampled = jnp.clip(jax.random.normal(value_key, (SEQ_TOKENS, MODEL_WIDTH), jnp.float32), -4.0, 4.0) * row_scale
    return sampled.astype(jnp.bfloat16)


def draw_key_states(key, part):
    key = jax.random.fold_in(key, 12)
    scale_key, value_key = jax.random.split(key)
    row_scale = jnp.exp(jax.random.uniform(scale_key, (SEQ_TOKENS, 1), jnp.float32, math.log(0.5), math.log(2.0)))
    sampled = jnp.clip(jax.random.normal(value_key, (SEQ_TOKENS, MODEL_WIDTH), jnp.float32), -4.0, 4.0) * row_scale
    return sampled.astype(jnp.bfloat16)


def draw_tile_pairs(key, part):
    key = jax.random.fold_in(key, 13)
    offsets = jnp.concatenate([jnp.arange(-TILE_REACH, 0), jnp.arange(1, TILE_REACH + 1)])
    row_keys = jax.random.split(key, TILE_COUNT)

    def shuffle_row(row_key):
        return jax.random.permutation(row_key, 2 * TILE_REACH)
    shuffled = jax.vmap(shuffle_row)(row_keys)
    place = jnp.arange(TILE_COUNT)[:, None]
    candidates = place + offsets[shuffled]
    inside = (candidates >= 0) & (candidates < TILE_COUNT)
    ranking = jnp.where(inside, 0, 1) * (2 * TILE_REACH) + jnp.arange(2 * TILE_REACH)[None, :]
    order = jnp.argsort(ranking, axis=1, stable=True)
    ranked = jnp.take_along_axis(candidates, order, axis=1)
    ranked_inside = jnp.take_along_axis(inside, order, axis=1)
    ranked = jnp.where(ranked_inside, ranked, place)
    return jnp.concatenate([place, ranked[:, :KEY_SLOTS - 1]], axis=1).astype(jnp.int32)


def draw_counts(key, part):
    key = jax.random.fold_in(key, 14)
    heavy_key, level_key, drop_key = jax.random.split(key, 3)
    regions = TILE_COUNT // TILES_DEV
    heavy = jax.random.randint(heavy_key, (regions,), 0, 4) == 0
    level = jnp.where(heavy, KEY_SLOTS, jax.random.randint(level_key, (regions,), 1, 3))
    per_tile = jnp.repeat(level, TILES_DEV, total_repeat_length=TILE_COUNT)
    wanted = jnp.maximum(1, per_tile - jax.random.randint(drop_key, (TILE_COUNT,), 0, 2))
    place = jnp.arange(TILE_COUNT)
    room = 1 + jnp.minimum(place, TILE_REACH) + jnp.minimum(TILE_COUNT - 1 - place, TILE_REACH)
    wanted = jnp.minimum(wanted, room)
    edge = min(KEY_SLOTS, 1 + TILE_REACH)
    wanted = wanted.at[TILE_COUNT // 2].set(KEY_SLOTS).at[TILE_COUNT // 4].set(1)
    wanted = wanted.at[0].set(edge).at[TILE_COUNT - 1].set(edge)
    return wanted.astype(jnp.int32)


def level_of(stream_key, dims, pieces, smallest, largest):
    factor_of = 1.0
    for axis_at, blocks in pieces:
        draws = jax.random.uniform(jax.random.fold_in(jax.random.fold_in(stream_key, 6), axis_at), (blocks,), jnp.float32, smallest / len(pieces), largest / len(pieces))
        factor_of = factor_of * jnp.repeat(jnp.exp(draws), dims[axis_at] // blocks).reshape((-1,) + (1,) * (len(dims) - 1 - axis_at))
    return factor_of


def noise(key, dims, scale, most, cuts=(), kind=jnp.bfloat16):
    values = jax.random.normal(key, dims, jnp.float32) * scale
    if len(cuts) > 0:
        values = level_of(key, dims, cuts, -0.22, 0.18) * values
    return jnp.clip(values, min=-most, max=most).astype(kind)


def setup_inputs(seed: int = 0, part: int = 0) -> dict:
    key_list = jax.random.split(jax.random.key(seed), 7)
    part_keys = jax.random.split(jax.random.fold_in(key_list[6], part), 7)
    return {
        "queries": draw_queries(jax.random.fold_in(jax.random.fold_in(key_list[6], part), 71), part),
        "key_states": draw_key_states(jax.random.fold_in(jax.random.fold_in(key_list[6], part), 71), part),
        "values": noise(part_keys[2], (SEQ_TOKENS, MODEL_WIDTH), 1.0, 6.0, ((0, 16),)),
        "grad_out": noise(part_keys[3], (SEQ_TOKENS, MODEL_WIDTH), 1.0, 6.0, ((0, 16),)),
        "tile_pairs": draw_tile_pairs(jax.random.fold_in(jax.random.fold_in(key_list[6], part), 71), part),
        "counts": draw_counts(jax.random.fold_in(jax.random.fold_in(key_list[6], part), 71), part),
    }


def rounded(block):
    return lax.optimization_barrier(block.astype(jnp.bfloat16)).astype(jnp.float32)


def reference(queries, key_states, values, grad_out, tile_pairs, counts):
    seq_tokens, width = queries.shape
    tile_total = seq_tokens // 128
    head_dim = width // HEAD_COUNT
    scale = head_dim ** -0.5
    query_blocks = queries.reshape(tile_total, 128, HEAD_COUNT, head_dim)
    key_blocks = key_states.reshape(tile_total, 128, HEAD_COUNT, head_dim)
    value_blocks = values.reshape(tile_total, 128, HEAD_COUNT, head_dim)
    grad_blocks = grad_out.reshape(tile_total, 128, HEAD_COUNT, head_dim)
    slot_ids = jnp.arange(tile_pairs.shape[1], dtype=jnp.int32)

    def one_tile(carry, tile_index):
        key_acc, value_acc = carry
        chosen = tile_pairs[tile_index]
        live = slot_ids < counts[tile_index]
        query_tile = query_blocks[tile_index].astype(jnp.float32)
        grad_tile = grad_blocks[tile_index].astype(jnp.float32)
        key_tiles = key_blocks[chosen].astype(jnp.float32)
        value_tiles = value_blocks[chosen].astype(jnp.float32)
        scores = jnp.einsum("qhd,skhd->hqsk", query_tile, key_tiles) * scale
        scores = jnp.where(live[None, None, :, None], scores, -jnp.inf)
        peak = jnp.max(scores, axis=(2, 3))
        logsum = peak + jnp.log(jnp.sum(jnp.exp(scores - peak[:, :, None, None]), axis=(2, 3)))
        probs = jnp.exp(scores - logsum[:, :, None, None])
        probs_low = rounded(probs)
        attended = jnp.einsum("hqsk,skhd->qhd", probs_low, value_tiles)
        row_delta = jnp.sum(grad_tile * attended, axis=2).T
        grad_probs = jnp.einsum("qhd,skhd->hqsk", grad_tile, value_tiles)
        grad_scores = rounded(probs * (grad_probs - row_delta[:, :, None, None]))
        grad_query = jnp.einsum("hqsk,skhd->qhd", grad_scores, key_tiles) * scale
        key_acc = key_acc.at[chosen].add(jnp.einsum("hqsk,qhd->skhd", grad_scores, query_tile))
        value_acc = value_acc.at[chosen].add(jnp.einsum("hqsk,qhd->skhd", probs_low, grad_tile))
        return (key_acc, value_acc), grad_query.astype(jnp.bfloat16)

    zeros = jnp.zeros((tile_total, 128, HEAD_COUNT, head_dim), jnp.float32)
    (key_acc, value_acc), grad_queries = lax.scan(one_tile, (zeros, zeros), jnp.arange(tile_total, dtype=jnp.int32))
    grad_queries = grad_queries.reshape(seq_tokens, width)
    grad_keys = (key_acc * scale).astype(jnp.bfloat16).reshape(seq_tokens, width)
    grad_values = value_acc.astype(jnp.bfloat16).reshape(seq_tokens, width)
    return grad_queries, grad_keys, grad_values
```

```python
import functools

import jax
import jax.numpy as jnp
from jax import lax
from jax.experimental import pallas as pl
from jax.experimental.pallas import tpu as pltpu
from jax.sharding import PartitionSpec as P

HEAD_DIM = 64
SCALE = HEAD_DIM ** (-0.5)
SCALE_LOG2 = SCALE * 1.4426950408889634
REACH = 2
BAND = 2 * REACH + 1
TILE = 128
PAIR = 2 * HEAD_DIM
DEAD = 1e30
CHUNKS = 2
F32 = jnp.float32
BF16 = jnp.bfloat16
NT = (((1,), (1,)), ((), ()))
VMEM_BYTES = 60 * 1024 * 1024


def merge(*sequences):
    items = []
    for place, sequence in enumerate(sequences):
        for at, emit in enumerate(sequence):
            items.append(((at + 0.5) / len(sequence), place, emit))
    items.sort(key=lambda item: item[:2])
    for _, _, emit in items:
        emit()


def by_head(x):
    first_head = lax.broadcasted_iota(jnp.int32, x.shape, 1) < HEAD_DIM
    zero = jnp.zeros_like(x)
    return jnp.concatenate([jnp.where(first_head, x, zero), jnp.where(first_head, zero, x)], axis=0)


def fill_dead(first, tiles, pairs, counts, dead):
    for n, t in enumerate(tiles):
        live = counts[first + t]
        for o in range(BAND):
            hit = jnp.int32(0)
            for s in range(pairs.shape[1]):
                same = (pairs[first + t, s] == first + t + o - REACH) & (s < live)
                hit = hit | same.astype(jnp.int32)
            dead[n, o] = jnp.where(hit > 0, 0.0, DEAD)


def key_rows(t, o):
    return slice((t + o) * TILE, (t + o + 1) * TILE)


def attend(tiles, q, do, k_ext, v_ext, kt, dead, bufs, add_value, add_key, put_query):
    qw, dw, s_buf, dp_buf, p_buf, ds_buf = bufs
    half = 32
    state = {}

    def scores(n):
        t, b, w = tiles[n], n % 2, n % 3

        def weights():
            rows = slice(t * TILE, (t + 1) * TILE)
            qw[w] = by_head(q[rows])
            dw[w] = by_head(do[rows])

        def one(o):
            def emit():
                here = slice(o * TILE, (o + 1) * TILE)
                s = lax.dot_general(k_ext[key_rows(t, o)], qw[w], NT, preferred_element_type=F32)
                s_buf[b, here] = s
                top = jnp.max(s.reshape(TILE // 8, 8, 2 * TILE), axis=0) - dead[n, o]
                state[n, "m"] = top if o == 0 else jnp.maximum(state[n, "m"], top)
                dp_buf[b, here] = lax.dot_general(
                    v_ext[key_rows(t, o)], dw[w], NT, preferred_element_type=F32
                )

            return emit

        return [weights] + [one(o) for o in range(BAND)]

    def softmax(n):
        b = n % 2

        def parts(o):
            return [slice(o * TILE + c, o * TILE + c + half) for c in range(0, TILE, half)]

        def fold(x):
            return jnp.sum(x.reshape(half // 8, 8, 2 * TILE), axis=0)

        def peak():
            state[n, "m"] = jnp.max(state[n, "m"], axis=0, keepdims=True) * SCALE_LOG2
            state[n, "l"] = jnp.zeros((8, 2 * TILE), F32)
            state[n, "d"] = jnp.zeros((8, 2 * TILE), F32)

        def powers(o):
            def emit():
                shift = state[n, "m"] + dead[n, o]
                for r in parts(o):
                    e = jnp.exp2(s_buf[b, r] * SCALE_LOG2 - shift)
                    s_buf[b, r] = e
                    state[n, "l"] = state[n, "l"] + fold(e)

            return emit

        def total():
            state[n, "r"] = 1.0 / jnp.sum(state[n, "l"], axis=0, keepdims=True)

        def normal(o):
            def emit():
                for r in parts(o):
                    p = s_buf[b, r] * state[n, "r"]
                    s_buf[b, r] = p
                    p_buf[b, r] = p.astype(BF16)
                    state[n, "d"] = state[n, "d"] + fold(p * dp_buf[b, r])

            return emit

        def delta():
            state[n, "d"] = jnp.sum(state[n, "d"], axis=0, keepdims=True)

        def score_grads(o):
            def emit():
                for r in parts(o):
                    ds_buf[b, r] = (s_buf[b, r] * (dp_buf[b, r] - state[n, "d"])).astype(BF16)

            return emit

        out = [peak] + [powers(o) for o in range(BAND)]
        out += [total] + [normal(o) for o in range(BAND)]
        return out + [delta] + [score_grads(o) for o in range(BAND)]

    def grads(n):
        t, b, w = tiles[n], n % 2, n % 3

        def one(o):
            def emit():
                here = slice(o * TILE, (o + 1) * TILE)
                add_value(n, t + o, jnp.dot(p_buf[b, here], dw[w], preferred_element_type=F32))
                add_key(n, t + o, jnp.dot(ds_buf[b, here], qw[w], preferred_element_type=F32))

            return emit

        def query():
            g = jnp.dot(
                kt[:, t * TILE : (t + BAND) * TILE], ds_buf[b], preferred_element_type=F32
            )
            first_head = lax.broadcasted_iota(jnp.int32, (PAIR, TILE), 0) < HEAD_DIM
            put_query(t, (jnp.where(first_head, g[:, :TILE], g[:, TILE:]).T * SCALE).astype(BF16))

        return [one(o) for o in range(BAND)] + [query]

    count = len(tiles)
    for step in range(count + 2):
        merge(
            scores(step) if step < count else [],
            softmax(step - 1) if 0 <= step - 1 < count else [],
            grads(step - 2) if 0 <= step - 2 < count else [],
        )


def work_buffers():
    band = BAND * TILE
    return [
        pltpu.VMEM((3, 2 * TILE, PAIR), BF16),
        pltpu.VMEM((3, 2 * TILE, PAIR), BF16),
        pltpu.VMEM((2, band, 2 * TILE), F32),
        pltpu.VMEM((2, band, 2 * TILE), F32),
        pltpu.VMEM((2, band, 2 * TILE), BF16),
        pltpu.VMEM((2, band, 2 * TILE), BF16),
    ]


def inner_kernel(tiles, first, pairs, counts, q, k, v, do, dq, dk, dv, kt, dead, *bufs):
    @pl.when(pl.program_id(0) == 0)
    def _():
        fill_dead(first[0], tiles, pairs, counts, dead)

    class Shifted:
        def __init__(self, ref):
            self.ref = ref

        def __getitem__(self, rows):
            return self.ref[rows.start - REACH * TILE : rows.stop - REACH * TILE]

    class ShiftedLanes:
        def __getitem__(self, at):
            return kt[:, at[1].start - REACH * TILE : at[1].stop - REACH * TILE]

    for j in range(k.shape[0] // TILE):
        rows = slice(j * TILE, (j + 1) * TILE)
        kt[:, rows] = k[rows].T

    def adder(out):
        def add(n, ext, x):
            rows = slice((ext - REACH) * TILE, (ext - REACH + 1) * TILE)
            if any(ext - BAND < t <= ext for t in tiles[:n]):
                x = out[rows] + x
            out[rows] = x

        return add

    def put(t, x):
        at = (t - tiles[0]) * TILE
        dq[at : at + TILE] = x

    attend(
        tiles, q, do, Shifted(k), Shifted(v), ShiftedLanes(), dead, bufs, adder(dv), adder(dk), put
    )


def edge_kernel(
    tiles, chained, first, pairs, counts, q, k, v, do, low, high, dq_mid, dk_mid, dv_mid, *rest
):
    rest = rest[3:] if chained else rest
    dq, dk, dv, to_low, to_high, k_ext, v_ext, kt, dk_acc, dv_acc, dead, *bufs = rest
    margin = REACH * TILE
    rows_dev = k.shape[0]
    tiles_dev = rows_dev // TILE

    @pl.when(pl.program_id(0) == 0)
    def _():
        fill_dead(first[0], tiles, pairs, counts, dead)

    for at, mine, ext in ((0, k, k_ext), (margin, v, v_ext)):
        ext[:margin] = low[at : at + margin]
        ext[margin : margin + rows_dev] = mine[...]
        ext[margin + rows_dev :] = high[at : at + margin]
    for j in range(tiles_dev + 2 * REACH):
        rows = slice(j * TILE, (j + 1) * TILE)
        kt[:, rows] = k_ext[rows].T

    def adder(acc, mid, out, at, scale):
        def add(n, ext, x):
            here = slice(ext * TILE, (ext + 1) * TILE)
            local = slice((ext - REACH) * TILE, (ext - REACH + 1) * TILE)
            inside = REACH <= ext < REACH + tiles_dev
            if any(ext - BAND < t <= ext for t in tiles[:n]):
                x = acc[here] + x
            elif inside:
                x = mid[local] + x
            if any(ext - BAND < t <= ext for t in tiles[n + 1 :]):
                acc[here] = x
                return
            x = (x * scale).astype(BF16)
            if inside:
                out[local] = x
            elif ext < REACH:
                to_low[at + ext * TILE : at + (ext + 1) * TILE] = x
            else:
                place = at + (ext - REACH - tiles_dev) * TILE
                to_high[place : place + TILE] = x

        return add

    def put(t, x):
        dq[t * TILE : (t + 1) * TILE] = x

    dq[margin : rows_dev - margin] = dq_mid[...]
    attend(
        tiles,
        q,
        do,
        k_ext,
        v_ext,
        kt,
        dead,
        bufs,
        adder(dv_acc, dv_mid, dv, margin, 1.0),
        adder(dk_acc, dk_mid, dk, 0, SCALE),
        put,
    )


def join_kernel(dk, dv, below, above, dk_out, dv_out):
    margin = REACH * TILE
    rows_dev = dk.shape[0]
    for mine, out, at in ((dk, dk_out, 0), (dv, dv_out, margin)):
        out[...] = mine[...]
        for rows, other in (
            (slice(0, margin), below),
            (slice(rows_dev - margin, rows_dev), above),
        ):
            out[rows] = (mine[rows].astype(F32) + other[at : at + margin].astype(F32)).astype(BF16)


def shards(queries, key_states, values, grad_out, tile_pairs, counts):
    rows_dev, width = queries.shape
    margin = REACH * TILE
    tiles_dev = rows_dev // TILE
    n_seq = lax.axis_size("seq")
    ahead = [(i, i + 1) for i in range(n_seq - 1)]
    back = [(i + 1, i) for i in range(n_seq - 1)]
    first = jnp.reshape(lax.axis_index("seq") * tiles_dev, (1,)).astype(jnp.int32)
    span = width // CHUNKS
    steps = span // PAIR
    params = pltpu.CompilerParams(vmem_limit_bytes=VMEM_BYTES)

    def pack(rows, columns):
        return jnp.concatenate([key_states[rows, columns], values[rows, columns]], axis=0)

    halos = []
    for c in range(CHUNKS):
        columns = slice(c * span, (c + 1) * span)
        low = lax.ppermute(pack(slice(rows_dev - margin, rows_dev), columns), "seq", ahead)
        high = lax.ppermute(pack(slice(0, margin), columns), "seq", back)
        halos.append((low, high))

    def block(rows, offset=0):
        return pl.BlockSpec((rows, PAIR), lambda h, *_: (0, offset + h))

    inner = tuple(range(REACH, tiles_dev - REACH))
    outer = tuple(range(REACH)) + tuple(range(tiles_dev - REACH, tiles_dev))
    pair_work = 5 * 2 * TILE * TILE * PAIR * BAND
    dq_mid, dk_mid, dv_mid = pl.pallas_call(
        functools.partial(inner_kernel, inner),
        grid_spec=pltpu.PrefetchScalarGridSpec(
            num_scalar_prefetch=3,
            grid=(width // PAIR,),
            in_specs=[block(rows_dev)] * 4,
            out_specs=[block(rows_dev - 2 * margin), block(rows_dev), block(rows_dev)],
            scratch_shapes=[
                pltpu.VMEM((PAIR, rows_dev), BF16),
                pltpu.SMEM((len(inner), BAND), F32),
            ]
            + work_buffers(),
        ),
        out_shape=[
            jax.ShapeDtypeStruct((rows_dev - 2 * margin, width), BF16),
            jax.ShapeDtypeStruct((rows_dev, width), F32),
            jax.ShapeDtypeStruct((rows_dev, width), F32),
        ],
        compiler_params=params,
        cost_estimate=pl.CostEstimate(
            flops=pair_work * len(inner) * (width // PAIR) * 8,
            bytes_accessed=12 * rows_dev * width,
            transcendentals=0,
        ),
        name="inner_tiles",
    )(first, tile_pairs, counts, queries, key_states, values, grad_out)

    ext_rows = rows_dev + 2 * margin
    outs = None
    sent = []
    for c, (low, high) in enumerate(halos):
        chained = outs is not None
        operands = [first, tile_pairs, counts, queries, key_states, values, grad_out, low, high]
        operands += [dq_mid, dk_mid, dv_mid]
        aliases = {}
        if chained:
            aliases = {len(operands) + i: i for i in range(3)}
            operands += outs
        at = c * steps
        *outs, to_low, to_high = pl.pallas_call(
            functools.partial(edge_kernel, outer, chained),
            grid_spec=pltpu.PrefetchScalarGridSpec(
                num_scalar_prefetch=3,
                grid=(steps,),
                in_specs=[block(rows_dev, at)] * 4
                + [block(2 * margin)] * 2
                + [block(rows_dev - 2 * margin, at), block(rows_dev, at), block(rows_dev, at)]
                + [pl.BlockSpec(memory_space=pl.ANY)] * (3 if chained else 0),
                out_specs=[block(rows_dev, at)] * 3 + [block(2 * margin)] * 2,
                scratch_shapes=[
                    pltpu.VMEM((ext_rows, PAIR), BF16),
                    pltpu.VMEM((ext_rows, PAIR), BF16),
                    pltpu.VMEM((PAIR, ext_rows), BF16),
                    pltpu.VMEM((ext_rows, PAIR), F32),
                    pltpu.VMEM((ext_rows, PAIR), F32),
                    pltpu.SMEM((len(outer), BAND), F32),
                ]
                + work_buffers(),
            ),
            out_shape=[jax.ShapeDtypeStruct((rows_dev, width), BF16)] * 3
            + [jax.ShapeDtypeStruct((2 * margin, span), BF16)] * 2,
            input_output_aliases=aliases,
            compiler_params=params,
            cost_estimate=pl.CostEstimate(
                flops=pair_work * len(outer) * steps * 8,
                bytes_accessed=20 * rows_dev * span,
                transcendentals=0,
            ),
            name="outer_tiles",
        )(*operands)
        sent.append((lax.ppermute(to_high, "seq", ahead), lax.ppermute(to_low, "seq", back)))

    grad_queries, grad_keys, grad_values = outs
    below = jnp.concatenate([low for low, _ in sent], axis=1)
    above = jnp.concatenate([high for _, high in sent], axis=1)
    grad_keys, grad_values = pl.pallas_call(
        join_kernel,
        grid=(width // 256,),
        in_specs=[
            pl.BlockSpec((rows_dev, 256), lambda h: (0, h)),
            pl.BlockSpec((rows_dev, 256), lambda h: (0, h)),
            pl.BlockSpec((2 * margin, 256), lambda h: (0, h)),
            pl.BlockSpec((2 * margin, 256), lambda h: (0, h)),
        ],
        out_specs=[pl.BlockSpec((rows_dev, 256), lambda h: (0, h))] * 2,
        out_shape=[jax.ShapeDtypeStruct((rows_dev, width), BF16)] * 2,
        input_output_aliases={0: 0, 1: 1},
        compiler_params=params,
        name="join_edges",
    )(grad_keys, grad_values, below, above)
    return (grad_queries, grad_keys, grad_values)


def solution(mesh):
    rows = P(("grp", "seq"), None)
    return jax.shard_map(
        shards,
        mesh=mesh,
        in_specs=(rows, rows, rows, rows, P("grp", None), P("grp")),
        out_specs=(rows, rows, rows),
        check_vma=False,
    )
```

```python
import functools

import jax
import jax.numpy as jnp
from jax import lax
from jax.experimental import pallas as pl
from jax.experimental.pallas import tpu as pltpu
from jax.sharding import PartitionSpec as P

HEAD_DIM = 64
SCALE = HEAD_DIM ** (-0.5)
SCALE_LOG2 = SCALE * 1.4426950408889634
REACH = 2
BAND = 2 * REACH + 1
TILE = 128
BLOCK = REACH * TILE
PAIR = 2 * HEAD_DIM
DEAD = 1e30
CHUNKS = 2
GROUP = 4
F32 = jnp.float32
BF16 = jnp.bfloat16
NT = (((1,), (1,)), ((), ()))
VMEM_BYTES = 60 * 1024 * 1024
KEYS = 3 * BLOCK
KEY_TILES = KEYS // TILE


def merge(*sequences):
    items = []
    for place, sequence in enumerate(sequences):
        for at, emit in enumerate(sequence):
            items.append(((at + 0.5) / len(sequence), place, emit))
    items.sort(key=lambda item: item[:2])
    for _, _, emit in items:
        emit()


def by_head(x):
    first_head = lax.broadcasted_iota(jnp.int32, x.shape, 1) < HEAD_DIM
    zero = jnp.zeros_like(x)
    return jnp.concatenate([jnp.where(first_head, x, zero), jnp.where(first_head, zero, x)], axis=0)


def fill_dead(tile, pairs, counts, dead):
    for n in range(REACH):
        live = counts[tile + n]
        for o in range(BAND):
            hit = jnp.int32(0)
            for s in range(pairs.shape[1]):
                same = (pairs[tile + n, s] == tile + n + o - REACH) & (s < live)
                hit = hit | same.astype(jnp.int32)
            dead[n, o] = jnp.where(hit > 0, 0.0, DEAD)


def attend(pairs_here, q, do, dq, k_ext, v_ext, kt, dk_acc, dv_acc, dead, bufs):
    qw, dw, s_buf, dp_buf, p_buf, ds_buf = bufs
    units = [(g, n) for g in range(pairs_here) for n in range(REACH)]
    half = 32
    state = {}

    def at(u):
        g, n = units[u]
        lanes = slice(g * PAIR, (g + 1) * PAIR)
        return g, n, lanes, slice(n * TILE, (n + 1) * TILE), slice(n * TILE, (n + BAND) * TILE)

    def scores(u):
        g, n, lanes, rows, band = at(u)
        b, w = u % 2, u % 3

        def weights():
            qw[w] = by_head(q[rows, lanes])
            dw[w] = by_head(do[rows, lanes])

        def product():
            state[u, "s"] = lax.dot_general(
                k_ext[band, lanes], qw[w], NT, preferred_element_type=F32
            )

        def one(o):
            def emit():
                here = slice(o * TILE, (o + 1) * TILE)
                s = state[u, "s"][here]
                s_buf[b, here] = s
                top = jnp.max(s.reshape(TILE // 8, 8, 2 * TILE), axis=0) - dead[n, o]
                state[u, "m"] = top if o == 0 else jnp.maximum(state[u, "m"], top)

            return emit

        def grad_probs():
            dp_buf[b] = lax.dot_general(v_ext[band, lanes], dw[w], NT, preferred_element_type=F32)

        return [weights, product] + [one(o) for o in range(BAND)] + [grad_probs]

    def softmax(u):
        n, b = units[u][1], u % 2

        def parts(o):
            return [slice(o * TILE + c, o * TILE + c + half) for c in range(0, TILE, half)]

        def fold(x):
            return jnp.sum(x.reshape(half // 8, 8, 2 * TILE), axis=0)

        def peak():
            state[u, "m"] = jnp.max(state[u, "m"], axis=0, keepdims=True) * SCALE_LOG2
            state[u, "l"] = jnp.zeros((8, 2 * TILE), F32)
            state[u, "d"] = jnp.zeros((8, 2 * TILE), F32)

        def powers(o):
            def emit():
                shift = state[u, "m"] + dead[n, o]
                for r in parts(o):
                    e = jnp.exp2(s_buf[b, r] * SCALE_LOG2 - shift)
                    s_buf[b, r] = e
                    state[u, "l"] = state[u, "l"] + fold(e)

            return emit

        def total():
            state[u, "r"] = 1.0 / jnp.sum(state[u, "l"], axis=0, keepdims=True)

        def normal(o):
            def emit():
                for r in parts(o):
                    p = s_buf[b, r] * state[u, "r"]
                    s_buf[b, r] = p
                    p_buf[b, r] = p.astype(BF16)
                    state[u, "d"] = state[u, "d"] + fold(p * dp_buf[b, r])

            return emit

        def delta():
            state[u, "d"] = jnp.sum(state[u, "d"], axis=0, keepdims=True)

        def score_grads(o):
            def emit():
                for r in parts(o):
                    ds_buf[b, r] = (s_buf[b, r] * (dp_buf[b, r] - state[u, "d"])).astype(BF16)

            return emit

        out = [peak] + [powers(o) for o in range(BAND)]
        out += [total] + [normal(o) for o in range(BAND)]
        return out + [delta] + [score_grads(o) for o in range(BAND)]

    def grads(u):
        g, n, lanes, rows, band = at(u)
        b, w = u % 2, u % 3

        def keyed(source, weight, acc):
            def emit():
                x = jnp.dot(source[b], weight[w], preferred_element_type=F32)
                if n == 0:
                    acc[band, lanes] = x
                else:
                    shared = slice(n * TILE, BAND * TILE)
                    acc[shared, lanes] = acc[shared, lanes] + x[: (BAND - n) * TILE]
                    acc[BAND * TILE :, lanes] = x[(BAND - n) * TILE :]

            return emit

        def query():
            x = jnp.dot(kt[g, :, band], ds_buf[b], preferred_element_type=F32)
            first_head = lax.broadcasted_iota(jnp.int32, (PAIR, TILE), 0) < HEAD_DIM
            dq[rows, lanes] = (
                jnp.where(first_head, x[:, :TILE], x[:, TILE:]).T * SCALE
            ).astype(BF16)

        return [keyed(p_buf, dw, dv_acc), query, keyed(ds_buf, qw, dk_acc)]

    count = len(units)
    for step in range(count + 2):
        merge(
            scores(step) if step < count else [],
            softmax(step - 1) if 0 <= step - 1 < count else [],
            grads(step - 2) if 0 <= step - 2 < count else [],
        )


def scratch(group):
    lanes, band = group * PAIR, BAND * TILE
    return [
        pltpu.VMEM((KEYS, lanes), BF16),
        pltpu.VMEM((KEYS, lanes), BF16),
        pltpu.VMEM((group, PAIR, KEYS), BF16),
        pltpu.VMEM((KEYS, lanes), F32),
        pltpu.VMEM((KEYS, lanes), F32),
        pltpu.SMEM((REACH, BAND), F32),
        pltpu.VMEM((3, 2 * TILE, PAIR), BF16),
        pltpu.VMEM((3, 2 * TILE, PAIR), BF16),
        pltpu.VMEM((2, band, 2 * TILE), F32),
        pltpu.VMEM((2, band, 2 * TILE), F32),
        pltpu.VMEM((2, band, 2 * TILE), BF16),
        pltpu.VMEM((2, band, 2 * TILE), BF16),
    ]


def transpose_keys(group, k_ext, kt):
    for g in range(group):
        for j in range(KEY_TILES):
            rows = slice(j * TILE, (j + 1) * TILE)
            kt[g, :, rows] = k_ext[rows, g * PAIR : (g + 1) * PAIR].T


def edge_kernel(group, chained, place, pairs, counts, q, do, k_near, k_mid, v_near, v_mid, halo, *rest):
    rest = rest[1:] if chained else rest
    dq, part_k, part_v, send, k_ext, v_ext, kt, dk_acc, dv_acc, dead, *bufs = rest
    low_edge = place[1] == 0
    outside = pl.multiple_of(jnp.where(low_edge, 0, 2 * BLOCK), BLOCK)
    inside = pl.multiple_of(jnp.where(low_edge, 2 * BLOCK, 0), BLOCK)

    @pl.when(pl.program_id(0) == 0)
    def _():
        fill_dead(place[0] + place[1] * REACH, pairs, counts, dead)

    for row, near, mid, ext in ((0, k_near, k_mid, k_ext), (BLOCK, v_near, v_mid, v_ext)):
        ext[pl.ds(outside, BLOCK)] = halo[row : row + BLOCK]
        ext[BLOCK : 2 * BLOCK] = near[...]
        ext[pl.ds(inside, BLOCK)] = mid[...]
    transpose_keys(group, k_ext, kt)
    attend(group, q, do, dq, k_ext, v_ext, kt, dk_acc, dv_acc, dead, bufs)
    for acc, part, row, scale in ((dk_acc, part_k, 0, SCALE), (dv_acc, part_v, BLOCK, 1.0)):
        send[row : row + BLOCK] = (acc[pl.ds(outside, BLOCK)] * scale).astype(BF16)
        part[:BLOCK] = acc[BLOCK : 2 * BLOCK]
        part[BLOCK:] = acc[pl.ds(inside, BLOCK)]


def inner_kernel(
    group, place, pairs, counts, q, do, k, v, chip_k, chip_v, cross_k, cross_v, back, dq_in, *rest
):
    dq, dk, dv, k_ext, v_ext, kt, dk_acc, dv_acc, dead, *bufs = rest
    cross = pl.multiple_of(place[1] * BLOCK, BLOCK)
    chip = pl.multiple_of(2 * BLOCK - cross, BLOCK)

    @pl.when(pl.program_id(0) == 0)
    def _():
        fill_dead(place[0] + REACH, pairs, counts, dead)

    transpose_keys(group, k, kt)
    attend(group, q, do, dq, k, v, kt, dk_acc, dv_acc, dead, bufs)
    for acc, part, other, row, out, scale in (
        (dk_acc, chip_k, cross_k, 0, dk, SCALE),
        (dv_acc, chip_v, cross_v, BLOCK, dv, 1.0),
    ):
        out[pl.ds(cross, BLOCK)] = ((acc[pl.ds(cross, BLOCK)] + other[:BLOCK]) * scale).astype(BF16)
        middle = acc[BLOCK : 2 * BLOCK] + part[BLOCK:] + other[BLOCK:]
        out[BLOCK : 2 * BLOCK] = (middle * scale).astype(BF16)
        edge = (acc[pl.ds(chip, BLOCK)] + part[:BLOCK]) * scale
        out[pl.ds(chip, BLOCK)] = (edge + back[row : row + BLOCK].astype(F32)).astype(BF16)


def join_kernel(place, dk, dv, back, dk_out, dv_out):
    dk_out[...] = (dk[...].astype(F32) + back[:BLOCK].astype(F32)).astype(BF16)
    dv_out[...] = (dv[...].astype(F32) + back[BLOCK:].astype(F32)).astype(BF16)


def shards(queries, key_states, values, grad_out, tile_pairs, counts):
    rows_dev, width = queries.shape
    tiles_dev = rows_dev // TILE
    n_seq = lax.axis_size("seq")
    me = lax.axis_index("seq")
    chip_swap = [(i, i ^ 1) for i in range(n_seq) if i ^ 1 < n_seq]
    cross_swap = [(i, i + 1) for i in range(1, n_seq - 1, 2)]
    cross_swap = cross_swap + [(b, a) for a, b in cross_swap]
    first = me * tiles_dev
    cross_block = jnp.where(me % 2 == 0, 0, 2)
    cross_place = jnp.stack([first, cross_block]).astype(jnp.int32)
    chip_place = jnp.stack([first, 2 - cross_block]).astype(jnp.int32)
    span = width // CHUNKS
    params = pltpu.CompilerParams(vmem_limit_bytes=VMEM_BYTES)
    cost = pl.CostEstimate(flops=1, bytes_accessed=1, transcendentals=0)

    def pack(block, columns):
        return jnp.concatenate(
            [
                lax.dynamic_slice_in_dim(x[:, columns], block * BLOCK, BLOCK, 0)
                for x in (key_states, values)
            ],
            axis=0,
        )

    chunks = [slice(c * span, (c + 1) * span) for c in range(CHUNKS)]
    chip_halo = lax.ppermute(pack(2 - cross_block, slice(0, width)), "seq", chip_swap)
    cross_halos = [lax.ppermute(pack(cross_block, c), "seq", cross_swap) for c in chunks]

    def edge(place, halo, column, lanes, dq):
        group = min(GROUP, lanes // PAIR)
        wide = group * PAIR
        at = column // wide

        def near(h, place, *_):
            return (place[1], at + h)

        def mid(h, *_):
            return (1, at + h)

        def own(h, *_):
            return (0, h)

        one = pl.BlockSpec((BLOCK, wide), near)
        two = pl.BlockSpec((BLOCK, wide), mid)
        double = pl.BlockSpec((2 * BLOCK, wide), own)
        operands = [place, tile_pairs, counts, queries, grad_out, key_states, key_states]
        operands += [values, values, halo]
        aliases = {}
        if dq is not None:
            aliases = {len(operands): 0}
            operands.append(dq)
        return pl.pallas_call(
            functools.partial(edge_kernel, group, dq is not None),
            grid_spec=pltpu.PrefetchScalarGridSpec(
                num_scalar_prefetch=3,
                grid=(lanes // wide,),
                in_specs=[one, one, one, two, one, two, double]
                + [pl.BlockSpec(memory_space=pl.ANY)] * len(aliases),
                out_specs=[one, double, double, double],
                scratch_shapes=scratch(group),
            ),
            out_shape=[
                jax.ShapeDtypeStruct((rows_dev, width), BF16),
                jax.ShapeDtypeStruct((2 * BLOCK, lanes), F32),
                jax.ShapeDtypeStruct((2 * BLOCK, lanes), F32),
                jax.ShapeDtypeStruct((2 * BLOCK, lanes), BF16),
            ],
            input_output_aliases=aliases,
            compiler_params=params,
            cost_estimate=cost,
            name="edge_tiles",
        )(*operands)

    dq, chip_k, chip_v, chip_send = edge(chip_place, chip_halo, 0, width, None)
    chip_back = lax.ppermute(chip_send, "seq", chip_swap)
    parts_k, parts_v, cross_back = [], [], []
    for c, halo in zip(chunks, cross_halos):
        dq, part_k, part_v, send = edge(cross_place, halo, c.start, span, dq)
        parts_k.append(part_k)
        parts_v.append(part_v)
        cross_back.append(lax.ppermute(send, "seq", cross_swap))

    wide = min(GROUP, span // PAIR) * PAIR
    grad_keys = grad_values = None
    for c, part_k, part_v in zip(chunks, parts_k, parts_v):
        at = c.start // wide

        def spec(rows, row, column):
            return pl.BlockSpec((rows, wide), lambda h, *_, row=row, column=column: (row, column + h))

        operands = [cross_place, tile_pairs, counts, queries, grad_out, key_states, values]
        operands += [chip_k, chip_v, part_k, part_v, chip_back, dq]
        aliases = {len(operands) - 1: 0}
        chained = []
        if grad_keys is not None:
            aliases |= {len(operands): 1, len(operands) + 1: 2}
            chained = [grad_keys, grad_values]

        def kernel(*refs, skip=len(chained)):
            head = len(operands)
            inner_kernel(wide // PAIR, *refs[:head], *refs[head + skip :])

        dq, grad_keys, grad_values = pl.pallas_call(
            kernel,
            grid_spec=pltpu.PrefetchScalarGridSpec(
                num_scalar_prefetch=3,
                grid=(span // wide,),
                in_specs=[spec(BLOCK, 1, at)] * 2
                + [spec(KEYS, 0, at)] * 2
                + [spec(2 * BLOCK, 0, at)] * 2
                + [spec(2 * BLOCK, 0, 0)] * 2
                + [spec(2 * BLOCK, 0, at)]
                + [pl.BlockSpec(memory_space=pl.ANY)] * (1 + len(chained)),
                out_specs=[spec(BLOCK, 1, at), spec(KEYS, 0, at), spec(KEYS, 0, at)],
                scratch_shapes=scratch(wide // PAIR),
            ),
            out_shape=[jax.ShapeDtypeStruct((rows_dev, width), BF16)] * 3,
            input_output_aliases=aliases,
            compiler_params=params,
            cost_estimate=cost,
            name="inner_tiles",
        )(*operands, *chained)

    for c, back in zip(chunks, cross_back):

        def edge_block(h, place, at=c.start // span):
            return (place[1], at)

        spec = pl.BlockSpec((BLOCK, span), edge_block)
        grad_keys, grad_values = pl.pallas_call(
            join_kernel,
            grid_spec=pltpu.PrefetchScalarGridSpec(
                num_scalar_prefetch=1,
                grid=(1,),
                in_specs=[spec, spec, pl.BlockSpec((2 * BLOCK, span), lambda h, *_: (0, 0))],
                out_specs=[spec, spec],
            ),
            out_shape=[jax.ShapeDtypeStruct((rows_dev, width), BF16)] * 2,
            input_output_aliases={1: 0, 2: 1},
            compiler_params=params,
            cost_estimate=cost,
            name="join_edges",
        )(cross_place, grad_keys, grad_values, back)
    return (dq, grad_keys, grad_values)


def solution(mesh):
    rows = P(("grp", "seq"), None)
    return jax.shard_map(
        shards,
        mesh=mesh,
        in_specs=(rows, rows, rows, rows, P("grp", None), P("grp")),
        out_specs=(rows, rows, rows),
        check_vma=False,
    )
```

```python
import functools

import jax
import jax.numpy as jnp
from jax import lax
from jax.experimental import pallas as pl
from jax.experimental.pallas import tpu as pltpu
from jax.sharding import PartitionSpec as P

HEAD_DIM = 64
SCALE = HEAD_DIM ** (-0.5)
SCALE_LOG2 = SCALE * 1.4426950408889634
REACH = 2
BAND = 2 * REACH + 1
TILE = 128
BLOCK = REACH * TILE
PAIR = 2 * HEAD_DIM
DEAD = 1e30
CHUNKS = 2
GROUP = 2
F32 = jnp.float32
BF16 = jnp.bfloat16
NT = (((1,), (1,)), ((), ()))
VMEM_BYTES = 63 * 1024 * 1024 + 768 * 1024
KEYS = 3 * BLOCK
KEY_TILES = KEYS // TILE


def merge(*sequences):
    items = []
    for place, sequence in enumerate(sequences):
        for at, emit in enumerate(sequence):
            items.append(((at + 0.5) / len(sequence), place, emit))
    items.sort(key=lambda item: item[:2])
    for _, _, emit in items:
        emit()


def by_head(x):
    first_head = lax.broadcasted_iota(jnp.int32, x.shape, 1) < HEAD_DIM
    zero = jnp.zeros_like(x)
    return jnp.concatenate([jnp.where(first_head, x, zero), jnp.where(first_head, zero, x)], axis=0)


def dead_slots(first, tiles_dev, tile_pairs, counts):
    chosen = lax.dynamic_slice_in_dim(tile_pairs, first, tiles_dev, 0)
    live = lax.dynamic_slice_in_dim(counts, first, tiles_dev, 0)
    own = first + jnp.arange(tiles_dev, dtype=jnp.int32)
    offset = jnp.arange(BAND, dtype=jnp.int32) - REACH
    slot = jnp.arange(tile_pairs.shape[1], dtype=jnp.int32)
    same = chosen[:, None, :] == (own[:, None] + offset[None, :])[:, :, None]
    hit = jnp.any(same & (slot[None, None, :] < live[:, None, None]), axis=2)
    return jnp.where(hit, 0.0, DEAD).astype(F32)


def attend(pairs_here, base, q, do, dq, k_ext, v_ext, kt, dk_acc, dv_acc, dead, bufs):
    qw, dw, s_buf, dp_buf, p_buf, ds_buf = bufs
    units = [(g, n) for g in range(pairs_here) for n in range(REACH)]
    half = 32
    state = {}

    def at(u):
        g, n = units[u]
        lanes = slice(g * PAIR, (g + 1) * PAIR)
        return g, n, lanes, slice(n * TILE, (n + 1) * TILE), slice(n * TILE, (n + BAND) * TILE)

    def scores(u):
        g, n, lanes, rows, band = at(u)
        b, w = u % 2, u % 3

        def weights():
            qw[w] = by_head(q[rows, lanes])
            dw[w] = by_head(do[rows, lanes])

        def product():
            state[u, "s"] = lax.dot_general(
                k_ext[band, lanes], qw[w], NT, preferred_element_type=F32
            )

        def one(o):
            def emit():
                here = slice(o * TILE, (o + 1) * TILE)
                s = state[u, "s"][here]
                s_buf[b, here] = s
                top = jnp.max(s.reshape(TILE // 8, 8, 2 * TILE), axis=0) - dead[base + n, o]
                state[u, "m"] = top if o == 0 else jnp.maximum(state[u, "m"], top)

            return emit

        def grad_probs():
            dp_buf[b] = lax.dot_general(v_ext[band, lanes], dw[w], NT, preferred_element_type=F32)

        return [weights, product] + [one(o) for o in range(BAND)] + [grad_probs]

    def softmax(u):
        n, b = units[u][1], u % 2

        def parts(o):
            return [slice(o * TILE + c, o * TILE + c + half) for c in range(0, TILE, half)]

        def fold(x):
            return jnp.sum(x.reshape(half // 8, 8, 2 * TILE), axis=0)

        def peak():
            state[u, "m"] = jnp.max(state[u, "m"], axis=0, keepdims=True) * SCALE_LOG2
            state[u, "l"] = jnp.zeros((8, 2 * TILE), F32)
            state[u, "d"] = jnp.zeros((8, 2 * TILE), F32)

        def powers(o):
            def emit():
                shift = state[u, "m"] + dead[base + n, o]
                for r in parts(o):
                    e = jnp.exp2(s_buf[b, r] * SCALE_LOG2 - shift)
                    s_buf[b, r] = e
                    state[u, "l"] = state[u, "l"] + fold(e)

            return emit

        def total():
            state[u, "r"] = 1.0 / jnp.sum(state[u, "l"], axis=0, keepdims=True)

        def normal(o):
            def emit():
                for r in parts(o):
                    p = s_buf[b, r] * state[u, "r"]
                    s_buf[b, r] = p
                    p_buf[b, r] = p.astype(BF16)
                    state[u, "d"] = state[u, "d"] + fold(p * dp_buf[b, r])

            return emit

        def delta():
            state[u, "d"] = jnp.sum(state[u, "d"], axis=0, keepdims=True)

        def score_grads(o):
            def emit():
                for r in parts(o):
                    ds_buf[b, r] = (s_buf[b, r] * (dp_buf[b, r] - state[u, "d"])).astype(BF16)

            return emit

        out = [peak] + [powers(o) for o in range(BAND)]
        out += [total] + [normal(o) for o in range(BAND)]
        return out + [delta] + [score_grads(o) for o in range(BAND)]

    def grads(u):
        g, n, lanes, rows, band = at(u)
        b, w = u % 2, u % 3

        def keyed(source, weight, acc):
            def emit():
                x = jnp.dot(source[b], weight[w], preferred_element_type=F32)
                if n == 0:
                    acc[band, lanes] = x
                else:
                    shared = slice(n * TILE, BAND * TILE)
                    acc[shared, lanes] = acc[shared, lanes] + x[: (BAND - n) * TILE]
                    acc[BAND * TILE :, lanes] = x[(BAND - n) * TILE :]

            return emit

        def query():
            x = jnp.dot(kt[g, :, band], ds_buf[b], preferred_element_type=F32)
            first_head = lax.broadcasted_iota(jnp.int32, (PAIR, TILE), 0) < HEAD_DIM
            dq[rows, lanes] = (
                jnp.where(first_head, x[:, :TILE], x[:, TILE:]).T * SCALE
            ).astype(BF16)

        return [keyed(p_buf, dw, dv_acc), query, keyed(ds_buf, qw, dk_acc)]

    count = len(units)
    for step in range(count + 2):
        merge(
            scores(step) if step < count else [],
            softmax(step - 1) if 0 <= step - 1 < count else [],
            grads(step - 2) if 0 <= step - 2 < count else [],
        )


def scratch(group):
    lanes, band = group * PAIR, BAND * TILE
    return [
        pltpu.VMEM((KEYS, lanes), BF16),
        pltpu.VMEM((KEYS, lanes), BF16),
        pltpu.VMEM((group, PAIR, KEYS), BF16),
        pltpu.VMEM((KEYS, lanes), F32),
        pltpu.VMEM((KEYS, lanes), F32),
        pltpu.VMEM((3, 2 * TILE, PAIR), BF16),
        pltpu.VMEM((3, 2 * TILE, PAIR), BF16),
        pltpu.VMEM((2, band, 2 * TILE), F32),
        pltpu.VMEM((2, band, 2 * TILE), F32),
        pltpu.VMEM((2, band, 2 * TILE), BF16),
        pltpu.VMEM((2, band, 2 * TILE), BF16),
    ]


def transpose_keys(group, k_ext, kt):
    for g in range(group):
        for j in range(KEY_TILES):
            rows = slice(j * TILE, (j + 1) * TILE)
            kt[g, :, rows] = k_ext[rows, g * PAIR : (g + 1) * PAIR].T


def edge_kernel(group, chained, place, dead, q, do, k_near, k_mid, v_near, v_mid, halo, *rest):
    rest = rest[chained:]
    dq, part_k, part_v, send, k_ext, v_ext, kt, dk_acc, dv_acc, *bufs = rest
    low_edge = place[0] == 0
    outside = pl.multiple_of(jnp.where(low_edge, 0, 2 * BLOCK), BLOCK)
    inside = pl.multiple_of(jnp.where(low_edge, 2 * BLOCK, 0), BLOCK)

    for row, near, mid, ext in ((0, k_near, k_mid, k_ext), (BLOCK, v_near, v_mid, v_ext)):
        ext[pl.ds(outside, BLOCK)] = halo[row : row + BLOCK]
        ext[BLOCK : 2 * BLOCK] = near[...]
        ext[pl.ds(inside, BLOCK)] = mid[...]
    transpose_keys(group, k_ext, kt)
    attend(group, place[0] * REACH, q, do, dq, k_ext, v_ext, kt, dk_acc, dv_acc, dead, bufs)
    for acc, part, row, scale in ((dk_acc, part_k, 0, SCALE), (dv_acc, part_v, BLOCK, 1.0)):
        send[row : row + BLOCK] = (acc[pl.ds(outside, BLOCK)] * scale).astype(BF16)
        part[:BLOCK] = acc[BLOCK : 2 * BLOCK]
        part[BLOCK:] = acc[pl.ds(inside, BLOCK)]


def inner_kernel(
    group, place, dead, q, do, k, v, chip_k, chip_v, cross_k, cross_v, back, dq_in, *rest
):
    dq, dk, dv, kt, dk_acc, dv_acc, *bufs = rest
    cross = pl.multiple_of(place[0] * BLOCK, BLOCK)
    chip = pl.multiple_of(2 * BLOCK - cross, BLOCK)

    transpose_keys(group, k, kt)
    attend(group, REACH, q, do, dq, k, v, kt, dk_acc, dv_acc, dead, bufs)
    for acc, part, other, row, out, scale in (
        (dk_acc, chip_k, cross_k, 0, dk, SCALE),
        (dv_acc, chip_v, cross_v, BLOCK, dv, 1.0),
    ):
        out[pl.ds(cross, BLOCK)] = ((acc[pl.ds(cross, BLOCK)] + other[:BLOCK]) * scale).astype(BF16)
        middle = acc[BLOCK : 2 * BLOCK] + part[BLOCK:] + other[BLOCK:]
        out[BLOCK : 2 * BLOCK] = (middle * scale).astype(BF16)
        edge = (acc[pl.ds(chip, BLOCK)] + part[:BLOCK]) * scale
        out[pl.ds(chip, BLOCK)] = (edge + back[row : row + BLOCK].astype(F32)).astype(BF16)


def join_kernel(place, dk, dv, *rest):
    *backs, dk_out, dv_out = rest
    span = backs[0].shape[1]
    for c, back in enumerate(backs):
        lanes = slice(c * span, (c + 1) * span)
        dk_out[:, lanes] = (dk[:, lanes].astype(F32) + back[:BLOCK].astype(F32)).astype(BF16)
        dv_out[:, lanes] = (dv[:, lanes].astype(F32) + back[BLOCK:].astype(F32)).astype(BF16)


def shards(queries, key_states, values, grad_out, tile_pairs, counts):
    rows_dev, width = queries.shape
    tiles_dev = rows_dev // TILE
    n_seq = lax.axis_size("seq")
    me = lax.axis_index("seq")
    chip_swap = [(i, i ^ 1) for i in range(n_seq) if i ^ 1 < n_seq]
    cross_swap = [(i, i + 1) for i in range(1, n_seq - 1, 2)]
    cross_swap = cross_swap + [(b, a) for a, b in cross_swap]
    first = me * tiles_dev
    cross_block = jnp.where(me % 2 == 0, 0, 2)
    cross_place = jnp.reshape(cross_block, (1,)).astype(jnp.int32)
    chip_place = jnp.reshape(2 - cross_block, (1,)).astype(jnp.int32)
    dead = dead_slots(first, tiles_dev, tile_pairs, counts)
    span = width // CHUNKS
    params = pltpu.CompilerParams(vmem_limit_bytes=VMEM_BYTES)
    cost = pl.CostEstimate(flops=1, bytes_accessed=1, transcendentals=0)

    def pack(block, columns):
        return jnp.concatenate(
            [
                lax.dynamic_slice_in_dim(x[:, columns], block * BLOCK, BLOCK, 0)
                for x in (key_states, values)
            ],
            axis=0,
        )

    chunks = [slice(c * span, (c + 1) * span) for c in range(CHUNKS)]
    cross_out = pack(cross_block, slice(0, width))
    cross_halo = lax.ppermute(cross_out, "seq", cross_swap)
    chip_halo = lax.ppermute(pack(2 - cross_block, slice(0, width)), "seq", chip_swap)

    def edge(place, halo, column, lanes, earlier):
        group = min(GROUP, lanes // PAIR)
        wide = group * PAIR
        at = column // wide

        def near(h, place, *_):
            return (place[0], at + h)

        def mid(h, *_):
            return (1, at + h)

        def own(h, *_):
            return (0, h)

        one = pl.BlockSpec((BLOCK, wide), near)
        two = pl.BlockSpec((BLOCK, wide), mid)
        double = pl.BlockSpec((2 * BLOCK, wide), own)
        halo_block = pl.BlockSpec((2 * BLOCK, wide), lambda h, *_: (0, at + h))
        operands = [place, dead, queries, grad_out, key_states, key_states]
        operands += [values, values, halo]
        aliases = {}
        for i, array in enumerate(earlier):
            if array is not None:
                aliases[len(operands)] = i
                operands.append(array)
        return pl.pallas_call(
            functools.partial(edge_kernel, group, len(aliases)),
            grid_spec=pltpu.PrefetchScalarGridSpec(
                num_scalar_prefetch=2,
                grid=(lanes // wide,),
                in_specs=[one, one, one, two, one, two, halo_block]
                + [pl.BlockSpec(memory_space=pl.ANY)] * len(aliases),
                out_specs=[one, halo_block, halo_block, double],
                scratch_shapes=scratch(group),
            ),
            out_shape=[
                jax.ShapeDtypeStruct((rows_dev, width), BF16),
                jax.ShapeDtypeStruct((2 * BLOCK, width), F32),
                jax.ShapeDtypeStruct((2 * BLOCK, width), F32),
                jax.ShapeDtypeStruct((2 * BLOCK, lanes), BF16),
            ],
            input_output_aliases=aliases,
            compiler_params=params,
            cost_estimate=cost,
            name="edge_tiles",
        )(*operands)

    dq, chip_k, chip_v, chip_send = edge(chip_place, chip_halo, 0, width, [None] * 3)
    chip_back = lax.ppermute(chip_send, "seq", chip_swap)
    cross_k = cross_v = None
    cross_back = []
    for c in chunks:
        dq, cross_k, cross_v, send = edge(
            cross_place, cross_halo, c.start, span, [dq, cross_k, cross_v]
        )
        cross_back.append(lax.ppermute(send, "seq", cross_swap))

    wide = GROUP * PAIR

    def spec(rows, row):
        return pl.BlockSpec((rows, wide), lambda h, *_: (row, h))

    operands = [cross_place, dead, queries, grad_out, key_states, values]
    operands += [chip_k, chip_v, cross_k, cross_v, chip_back, dq]
    dq, grad_keys, grad_values = pl.pallas_call(
        functools.partial(inner_kernel, GROUP),
        grid_spec=pltpu.PrefetchScalarGridSpec(
            num_scalar_prefetch=2,
            grid=(width // wide,),
            in_specs=[spec(BLOCK, 1)] * 2
            + [spec(KEYS, 0)] * 2
            + [spec(2 * BLOCK, 0)] * 5
            + [pl.BlockSpec(memory_space=pl.ANY)],
            out_specs=[spec(BLOCK, 1), spec(KEYS, 0), spec(KEYS, 0)],
            scratch_shapes=scratch(GROUP)[2:],
        ),
        out_shape=[jax.ShapeDtypeStruct((rows_dev, width), BF16)] * 3,
        input_output_aliases={len(operands) - 1: 0},
        compiler_params=params,
        cost_estimate=cost,
        name="inner_tiles",
    )(*operands)

    edge_spec = pl.BlockSpec((BLOCK, width), lambda h, place: (place[0], 0))
    grad_keys, grad_values = pl.pallas_call(
        join_kernel,
        grid_spec=pltpu.PrefetchScalarGridSpec(
            num_scalar_prefetch=1,
            grid=(1,),
            in_specs=[edge_spec] * 2
            + [pl.BlockSpec((2 * BLOCK, span), lambda h, *_: (0, 0))] * CHUNKS,
            out_specs=[edge_spec] * 2,
        ),
        out_shape=[jax.ShapeDtypeStruct((rows_dev, width), BF16)] * 2,
        input_output_aliases={1: 0, 2: 1},
        compiler_params=params,
        cost_estimate=cost,
        name="join_edges",
    )(cross_place, grad_keys, grad_values, *cross_back)
    return (dq, grad_keys, grad_values)


def solution(mesh):
    rows = P(("grp", "seq"), None)
    return jax.shard_map(
        shards,
        mesh=mesh,
        in_specs=(rows, rows, rows, rows, P("grp", None), P("grp")),
        out_specs=(rows, rows, rows),
        check_vma=False,
    )
```

```python
import functools

import jax
import jax.numpy as jnp
from jax import lax
from jax.experimental import pallas as pl
from jax.experimental.pallas import tpu as pltpu
from jax.sharding import PartitionSpec as P

HEAD_DIM = 64
SCALE = HEAD_DIM ** (-0.5)
SCALE_LOG2 = SCALE * 1.4426950408889634
REACH = 2
BAND = 2 * REACH + 1
TILE = 128
BLOCK = REACH * TILE
PAIR = 2 * HEAD_DIM
DEAD = 1e30
CHUNKS = 2
GROUP = 2
WEIGHTS = 6
F32 = jnp.float32
BF16 = jnp.bfloat16
NT = (((1,), (1,)), ((), ()))
VMEM_BYTES = 63 * 1024 * 1024 + 768 * 1024
KEYS = 3 * BLOCK
KEY_TILES = KEYS // TILE


def merge(*sequences):
    items = []
    for place, sequence in enumerate(sequences):
        for at, emit in enumerate(sequence):
            items.append(((at + 0.5) / len(sequence), place, emit))
    items.sort(key=lambda item: item[:2])
    for _, _, emit in items:
        emit()


def by_head(x):
    x = x.T
    first_head = lax.broadcasted_iota(jnp.int32, x.shape, 0) < HEAD_DIM
    zero = jnp.zeros_like(x)
    return jnp.concatenate([jnp.where(first_head, x, zero), jnp.where(first_head, zero, x)], axis=1)


def dead_slots(first, tiles_dev, tile_pairs, counts):
    chosen = lax.dynamic_slice_in_dim(tile_pairs, first, tiles_dev, 0)
    live = lax.dynamic_slice_in_dim(counts, first, tiles_dev, 0)
    own = first + jnp.arange(tiles_dev, dtype=jnp.int32)
    offset = jnp.arange(BAND, dtype=jnp.int32) - REACH
    slot = jnp.arange(tile_pairs.shape[1], dtype=jnp.int32)
    same = chosen[:, None, :] == (own[:, None] + offset[None, :])[:, :, None]
    hit = jnp.any(same & (slot[None, None, :] < live[:, None, None]), axis=2)
    return jnp.where(hit, 0.0, DEAD).astype(F32)


def attend(pairs_here, base, q, do, dq, k_ext, v_ext, kt, dk_acc, dv_acc, dead, bufs):
    qw, dw, s_buf, dp_buf, e_buf, ds_buf = bufs
    units = [(g, n) for g in range(pairs_here) for n in range(REACH)]
    half = 32
    state = {}

    def at(u):
        g, n = units[u]
        lanes = slice(g * PAIR, (g + 1) * PAIR)
        return g, n, lanes, slice(n * TILE, (n + 1) * TILE), slice(n * TILE, (n + BAND) * TILE)

    def scores(u):
        g, n, lanes, rows, band = at(u)
        b, w = u % 2, u % WEIGHTS

        def weights():
            qw[w] = by_head(q[rows, lanes])
            dw[w] = by_head(do[rows, lanes])

        def product():
            state[u, "s"] = jnp.dot(k_ext[band, lanes], qw[w], preferred_element_type=F32)

        def one(o):
            def emit():
                here = slice(o * TILE, (o + 1) * TILE)
                s = state[u, "s"][here]
                s_buf[b, here] = s
                top = jnp.max(s.reshape(TILE // 8, 8, 2 * TILE), axis=0) - dead[base + n, o]
                state[u, "m"] = top if o == 0 else jnp.maximum(state[u, "m"], top)

            return emit

        def grad_probs():
            dp_buf[b] = jnp.dot(v_ext[band, lanes], dw[w], preferred_element_type=F32)

        return [weights, product] + [one(o) for o in range(BAND)] + [grad_probs]

    def softmax(u):
        g, n, lanes, rows, band = at(u)
        b, wide = u % 2, slice(n * 2 * TILE, (n + 1) * 2 * TILE)

        def parts(o):
            return [slice(o * TILE + c, o * TILE + c + half) for c in range(0, TILE, half)]

        def shifted(r):
            return slice(r.start + n * TILE, r.stop + n * TILE)

        def fold(x):
            return jnp.sum(x.reshape(half // 8, 8, 2 * TILE), axis=0)

        def peak():
            state[u, "m"] = jnp.max(state[u, "m"], axis=0, keepdims=True) * SCALE_LOG2
            state[u, "l"] = jnp.zeros((8, 2 * TILE), F32)
            state[u, "d"] = jnp.zeros((8, 2 * TILE), F32)

        def powers(o):
            def emit():
                shift = state[u, "m"] + dead[base + n, o]
                for r in parts(o):
                    e = jnp.exp2(s_buf[b, r] * SCALE_LOG2 - shift)
                    s_buf[b, r] = e
                    e_buf[g % 2, shifted(r), wide] = e.astype(BF16)
                    state[u, "l"] = state[u, "l"] + fold(e)
                    state[u, "d"] = state[u, "d"] + fold(e * dp_buf[b, r])

            return emit

        def total():
            r = 1.0 / jnp.sum(state[u, "l"], axis=0, keepdims=True)
            state[u, "r"] = r
            state[u, "d"] = jnp.sum(state[u, "d"], axis=0, keepdims=True) * r

        def score_grads(o):
            def emit():
                for r in parts(o):
                    ds = s_buf[b, r] * (dp_buf[b, r] - state[u, "d"])
                    ds_buf[g % 2, shifted(r), wide] = ds.astype(BF16)

            return emit

        return (
            [peak]
            + [powers(o) for o in range(BAND)]
            + [total]
            + [score_grads(o) for o in range(BAND)]
        )

    def query_grads(u):
        g, n, lanes, rows, band = at(u)
        wide = slice(n * 2 * TILE, (n + 1) * 2 * TILE)

        def emit():
            x = jnp.dot(kt[g, :, band], ds_buf[g % 2, band, wide], preferred_element_type=F32)
            x = x * (state[u, "r"] * SCALE)
            first_head = lax.broadcasted_iota(jnp.int32, (PAIR, TILE), 0) < HEAD_DIM
            dq[rows, lanes] = jnp.where(first_head, x[:, :TILE], x[:, TILE:]).T.astype(BF16)

        return [emit]

    def key_grads(g, source, weight, acc):
        lanes = slice(g * PAIR, (g + 1) * PAIR)
        both = slice(0, 4 * TILE)

        def scaled():
            state[g, "w"] = jnp.concatenate(
                [
                    (weight[u % WEIGHTS].astype(F32) * state[u, "r"]).astype(BF16)
                    for u in (REACH * g, REACH * g + 1)
                ],
                axis=1,
            )

        def rows_of(rows, wide):
            def emit():
                acc[rows, lanes] = lax.dot_general(
                    source[g % 2, rows, wide],
                    state[g, "w"][:, wide],
                    NT,
                    preferred_element_type=F32,
                )

            return emit

        return [
            scaled,
            rows_of(slice(0, TILE), slice(0, 2 * TILE)),
            rows_of(slice(TILE, BAND * TILE), both),
            rows_of(slice(BAND * TILE, KEYS), slice(2 * TILE, 4 * TILE)),
        ]

    count = len(units)
    for step in range(count + 3):
        late = []
        if 0 <= step - 2 < count:
            late += query_grads(step - 2)
        g, odd = divmod(step - 3, 2)
        if 0 <= g < pairs_here:
            late += key_grads(g, *((ds_buf, qw, dk_acc) if odd else (e_buf, dw, dv_acc)))
        merge(
            scores(step) if step < count else [],
            softmax(step - 1) if 0 <= step - 1 < count else [],
            late,
        )


def scratch(group):
    lanes, band = group * PAIR, BAND * TILE
    return [
        pltpu.VMEM((KEYS, lanes), BF16),
        pltpu.VMEM((KEYS, lanes), BF16),
        pltpu.VMEM((group, PAIR, KEYS), BF16),
        pltpu.VMEM((KEYS, lanes), F32),
        pltpu.VMEM((KEYS, lanes), F32),
        pltpu.VMEM((WEIGHTS, PAIR, 2 * TILE), BF16),
        pltpu.VMEM((WEIGHTS, PAIR, 2 * TILE), BF16),
        pltpu.VMEM((2, band, 2 * TILE), F32),
        pltpu.VMEM((2, band, 2 * TILE), F32),
        pltpu.VMEM((2, KEYS, 4 * TILE), BF16),
        pltpu.VMEM((2, KEYS, 4 * TILE), BF16),
    ]


def transpose_keys(group, k_ext, kt):
    for g in range(group):
        for j in range(KEY_TILES):
            rows = slice(j * TILE, (j + 1) * TILE)
            kt[g, :, rows] = k_ext[rows, g * PAIR : (g + 1) * PAIR].T


def edge_kernel(group, chained, place, dead, q, do, k_near, k_mid, v_near, v_mid, halo, *rest):
    rest = rest[chained:]
    dq, part_k, part_v, send, k_ext, v_ext, kt, dk_acc, dv_acc, *bufs = rest
    low_edge = place[0] == 0
    outside = pl.multiple_of(jnp.where(low_edge, 0, 2 * BLOCK), BLOCK)
    inside = pl.multiple_of(jnp.where(low_edge, 2 * BLOCK, 0), BLOCK)

    for row, near, mid, ext in ((0, k_near, k_mid, k_ext), (BLOCK, v_near, v_mid, v_ext)):
        ext[pl.ds(outside, BLOCK)] = halo[row : row + BLOCK]
        ext[BLOCK : 2 * BLOCK] = near[...]
        ext[pl.ds(inside, BLOCK)] = mid[...]
    transpose_keys(group, k_ext, kt)
    attend(group, place[0] * REACH, q, do, dq, k_ext, v_ext, kt, dk_acc, dv_acc, dead, bufs)
    for acc, part, row, scale in ((dk_acc, part_k, 0, SCALE), (dv_acc, part_v, BLOCK, 1.0)):
        send[row : row + BLOCK] = (acc[pl.ds(outside, BLOCK)] * scale).astype(BF16)
        part[:BLOCK] = acc[BLOCK : 2 * BLOCK]
        part[BLOCK:] = acc[pl.ds(inside, BLOCK)]


def inner_kernel(
    group, place, dead, q, do, k, v, chip_k, chip_v, cross_k, cross_v, back, dq_in, *rest
):
    dq, dk, dv, kt, dk_acc, dv_acc, *bufs = rest
    cross = pl.multiple_of(place[0] * BLOCK, BLOCK)
    chip = pl.multiple_of(2 * BLOCK - cross, BLOCK)

    transpose_keys(group, k, kt)
    attend(group, REACH, q, do, dq, k, v, kt, dk_acc, dv_acc, dead, bufs)
    for acc, part, other, row, out, scale in (
        (dk_acc, chip_k, cross_k, 0, dk, SCALE),
        (dv_acc, chip_v, cross_v, BLOCK, dv, 1.0),
    ):
        out[pl.ds(cross, BLOCK)] = ((acc[pl.ds(cross, BLOCK)] + other[:BLOCK]) * scale).astype(BF16)
        middle = acc[BLOCK : 2 * BLOCK] + part[BLOCK:] + other[BLOCK:]
        out[BLOCK : 2 * BLOCK] = (middle * scale).astype(BF16)
        edge = (acc[pl.ds(chip, BLOCK)] + part[:BLOCK]) * scale
        out[pl.ds(chip, BLOCK)] = (edge + back[row : row + BLOCK].astype(F32)).astype(BF16)


def join_kernel(place, dk, dv, *rest):
    *backs, dk_out, dv_out = rest
    span = backs[0].shape[1]
    for c, back in enumerate(backs):
        lanes = slice(c * span, (c + 1) * span)
        dk_out[:, lanes] = (dk[:, lanes].astype(F32) + back[:BLOCK].astype(F32)).astype(BF16)
        dv_out[:, lanes] = (dv[:, lanes].astype(F32) + back[BLOCK:].astype(F32)).astype(BF16)


def shards(queries, key_states, values, grad_out, tile_pairs, counts):
    rows_dev, width = queries.shape
    tiles_dev = rows_dev // TILE
    n_seq = lax.axis_size("seq")
    me = lax.axis_index("seq")
    chip_swap = [(i, i ^ 1) for i in range(n_seq) if i ^ 1 < n_seq]
    cross_swap = [(i, i + 1) for i in range(1, n_seq - 1, 2)]
    cross_swap = cross_swap + [(b, a) for a, b in cross_swap]
    first = me * tiles_dev
    cross_block = jnp.where(me % 2 == 0, 0, 2)
    cross_place = jnp.reshape(cross_block, (1,)).astype(jnp.int32)
    chip_place = jnp.reshape(2 - cross_block, (1,)).astype(jnp.int32)
    dead = dead_slots(first, tiles_dev, tile_pairs, counts)
    span = width // CHUNKS
    params = pltpu.CompilerParams(vmem_limit_bytes=VMEM_BYTES)
    cost = pl.CostEstimate(flops=1, bytes_accessed=1, transcendentals=0)

    def pack(block, columns):
        return jnp.concatenate(
            [
                lax.dynamic_slice_in_dim(x[:, columns], block * BLOCK, BLOCK, 0)
                for x in (key_states, values)
            ],
            axis=0,
        )

    chunks = [slice(c * span, (c + 1) * span) for c in range(CHUNKS)]
    cross_out = pack(cross_block, slice(0, width))
    cross_halo = lax.ppermute(cross_out, "seq", cross_swap)
    chip_halo = lax.ppermute(pack(2 - cross_block, slice(0, width)), "seq", chip_swap)

    def edge(place, halo, column, lanes, earlier):
        group = min(GROUP, lanes // PAIR)
        wide = group * PAIR
        at = column // wide

        def near(h, place, *_):
            return (place[0], at + h)

        def mid(h, *_):
            return (1, at + h)

        def own(h, *_):
            return (0, h)

        one = pl.BlockSpec((BLOCK, wide), near)
        two = pl.BlockSpec((BLOCK, wide), mid)
        double = pl.BlockSpec((2 * BLOCK, wide), own)
        halo_block = pl.BlockSpec((2 * BLOCK, wide), lambda h, *_: (0, at + h))
        operands = [place, dead, queries, grad_out, key_states, key_states]
        operands += [values, values, halo]
        aliases = {}
        for i, array in enumerate(earlier):
            if array is not None:
                aliases[len(operands)] = i
                operands.append(array)
        return pl.pallas_call(
            functools.partial(edge_kernel, group, len(aliases)),
            grid_spec=pltpu.PrefetchScalarGridSpec(
                num_scalar_prefetch=2,
                grid=(lanes // wide,),
                in_specs=[one, one, one, two, one, two, halo_block]
                + [pl.BlockSpec(memory_space=pl.ANY)] * len(aliases),
                out_specs=[one, halo_block, halo_block, double],
                scratch_shapes=scratch(group),
            ),
            out_shape=[
                jax.ShapeDtypeStruct((rows_dev, width), BF16),
                jax.ShapeDtypeStruct((2 * BLOCK, width), F32),
                jax.ShapeDtypeStruct((2 * BLOCK, width), F32),
                jax.ShapeDtypeStruct((2 * BLOCK, lanes), BF16),
            ],
            input_output_aliases=aliases,
            compiler_params=params,
            cost_estimate=cost,
            name="edge_tiles",
        )(*operands)

    dq, chip_k, chip_v, chip_send = edge(chip_place, chip_halo, 0, width, [None] * 3)
    chip_back = lax.ppermute(chip_send, "seq", chip_swap)
    cross_k = cross_v = None
    cross_back = []
    for c in chunks:
        dq, cross_k, cross_v, send = edge(
            cross_place, cross_halo, c.start, span, [dq, cross_k, cross_v]
        )
        cross_back.append(lax.ppermute(send, "seq", cross_swap))

    wide = GROUP * PAIR

    def spec(rows, row):
        return pl.BlockSpec((rows, wide), lambda h, *_: (row, h))

    operands = [cross_place, dead, queries, grad_out, key_states, values]
    operands += [chip_k, chip_v, cross_k, cross_v, chip_back, dq]
    dq, grad_keys, grad_values = pl.pallas_call(
        functools.partial(inner_kernel, GROUP),
        grid_spec=pltpu.PrefetchScalarGridSpec(
            num_scalar_prefetch=2,
            grid=(width // wide,),
            in_specs=[spec(BLOCK, 1)] * 2
            + [spec(KEYS, 0)] * 2
            + [spec(2 * BLOCK, 0)] * 5
            + [pl.BlockSpec(memory_space=pl.ANY)],
            out_specs=[spec(BLOCK, 1), spec(KEYS, 0), spec(KEYS, 0)],
            scratch_shapes=scratch(GROUP)[2:],
        ),
        out_shape=[jax.ShapeDtypeStruct((rows_dev, width), BF16)] * 3,
        input_output_aliases={len(operands) - 1: 0},
        compiler_params=params,
        cost_estimate=cost,
        name="inner_tiles",
    )(*operands)

    edge_spec = pl.BlockSpec((BLOCK, width), lambda h, place: (place[0], 0))
    grad_keys, grad_values = pl.pallas_call(
        join_kernel,
        grid_spec=pltpu.PrefetchScalarGridSpec(
            num_scalar_prefetch=1,
            grid=(1,),
            in_specs=[edge_spec] * 2
            + [pl.BlockSpec((2 * BLOCK, span), lambda h, *_: (0, 0))] * CHUNKS,
            out_specs=[edge_spec] * 2,
        ),
        out_shape=[jax.ShapeDtypeStruct((rows_dev, width), BF16)] * 2,
        input_output_aliases={1: 0, 2: 1},
        compiler_params=params,
        cost_estimate=cost,
        name="join_edges",
    )(cross_place, grad_keys, grad_values, *cross_back)
    return (dq, grad_keys, grad_values)


def solution(mesh):
    rows = P(("grp", "seq"), None)
    return jax.shard_map(
        shards,
        mesh=mesh,
        in_specs=(rows, rows, rows, rows, P("grp", None), P("grp")),
        out_specs=(rows, rows, rows),
        check_vma=False,
    )
```

```python
import functools

import jax
import jax.numpy as jnp
from jax import lax
from jax.experimental import pallas as pl
from jax.experimental.pallas import tpu as pltpu
from jax.sharding import PartitionSpec as P

HEAD_DIM = 64
SCALE = HEAD_DIM ** (-0.5)
SCALE_LOG2 = SCALE * 1.4426950408889634
REACH = 2
BAND = 2 * REACH + 1
TILE = 128
BLOCK = REACH * TILE
PAIR = 2 * HEAD_DIM
DEAD = 1e30
CUTS = (0, 4, 8)
GROUP = 2
WEIGHTS = 6
F32 = jnp.float32
BF16 = jnp.bfloat16
NT = (((1,), (1,)), ((), ()))
VMEM_BYTES = 63 * 1024 * 1024 + 768 * 1024
KEYS = 3 * BLOCK
KEY_TILES = KEYS // TILE


def merge(*sequences):
    items = []
    for place, sequence in enumerate(sequences):
        for at, emit in enumerate(sequence):
            items.append(((at + 0.5) / len(sequence), place, emit))
    items.sort(key=lambda item: item[:2])
    for _, _, emit in items:
        emit()


def by_head(x):
    x = x.T
    first_head = lax.broadcasted_iota(jnp.int32, x.shape, 0) < HEAD_DIM
    zero = jnp.zeros_like(x)
    return jnp.concatenate([jnp.where(first_head, x, zero), jnp.where(first_head, zero, x)], axis=1)


def dead_slots(first, tiles_dev, tile_pairs, counts):
    chosen = lax.dynamic_slice_in_dim(tile_pairs, first, tiles_dev, 0)
    live = lax.dynamic_slice_in_dim(counts, first, tiles_dev, 0)
    own = first + jnp.arange(tiles_dev, dtype=jnp.int32)
    offset = jnp.arange(BAND, dtype=jnp.int32) - REACH
    slot = jnp.arange(tile_pairs.shape[1], dtype=jnp.int32)
    same = chosen[:, None, :] == (own[:, None] + offset[None, :])[:, :, None]
    hit = jnp.any(same & (slot[None, None, :] < live[:, None, None]), axis=2)
    return jnp.where(hit, 0.0, DEAD).astype(F32)


def attend(pairs_here, base, q, do, dq, k_ext, v_ext, kt, dk_acc, dv_acc, dead, bufs, finish):
    qw, dw, s_buf, dp_buf, e_buf, ds_buf = bufs
    units = [(g, n) for g in range(pairs_here) for n in range(REACH)]
    half = 32
    state = {}

    def at(u):
        g, n = units[u]
        lanes = slice(g * PAIR, (g + 1) * PAIR)
        return g, n, lanes, slice(n * TILE, (n + 1) * TILE), slice(n * TILE, (n + BAND) * TILE)

    def scores(u):
        g, n, lanes, rows, band = at(u)
        b, w = u % 2, u % WEIGHTS

        def weights():
            qw[w] = by_head(q[rows, lanes])
            dw[w] = by_head(do[rows, lanes])

        def product():
            state[u, "s"] = jnp.dot(k_ext[band, lanes], qw[w], preferred_element_type=F32)

        def one(o):
            def emit():
                here = slice(o * TILE, (o + 1) * TILE)
                s = state[u, "s"][here]
                s_buf[b, here] = s
                top = jnp.max(s.reshape(TILE // 8, 8, 2 * TILE), axis=0) - dead[base + n, o]
                state[u, "m"] = top if o == 0 else jnp.maximum(state[u, "m"], top)

            return emit

        def grad_probs():
            dp_buf[b] = jnp.dot(v_ext[band, lanes], dw[w], preferred_element_type=F32)

        return [weights, product] + [one(o) for o in range(BAND)] + [grad_probs]

    def softmax(u):
        g, n, lanes, rows, band = at(u)
        b, wide = u % 2, slice(n * 2 * TILE, (n + 1) * 2 * TILE)

        def parts(o):
            return [slice(o * TILE + c, o * TILE + c + half) for c in range(0, TILE, half)]

        def shifted(r):
            return slice(r.start + n * TILE, r.stop + n * TILE)

        def fold(x):
            return jnp.sum(x.reshape(half // 8, 8, 2 * TILE), axis=0)

        def peak():
            state[u, "m"] = jnp.max(state[u, "m"], axis=0, keepdims=True) * SCALE_LOG2
            state[u, "l"] = jnp.zeros((8, 2 * TILE), F32)
            state[u, "d"] = jnp.zeros((8, 2 * TILE), F32)

        def powers(o):
            def emit():
                shift = state[u, "m"] + dead[base + n, o]
                for r in parts(o):
                    e = jnp.exp2(s_buf[b, r] * SCALE_LOG2 - shift)
                    s_buf[b, r] = e
                    e_buf[g % 2, shifted(r), wide] = e.astype(BF16)
                    state[u, "l"] = state[u, "l"] + fold(e)
                    state[u, "d"] = state[u, "d"] + fold(e * dp_buf[b, r])

            return emit

        def total():
            r = 1.0 / jnp.sum(state[u, "l"], axis=0, keepdims=True)
            state[u, "r"] = r
            state[u, "d"] = jnp.sum(state[u, "d"], axis=0, keepdims=True) * r

        def score_grads(o):
            def emit():
                for r in parts(o):
                    ds = s_buf[b, r] * (dp_buf[b, r] - state[u, "d"])
                    ds_buf[g % 2, shifted(r), wide] = ds.astype(BF16)

            return emit

        return (
            [peak]
            + [powers(o) for o in range(BAND)]
            + [total]
            + [score_grads(o) for o in range(BAND)]
        )

    def query_grads(u):
        g, n, lanes, rows, band = at(u)
        wide = slice(n * 2 * TILE, (n + 1) * 2 * TILE)

        def emit():
            x = jnp.dot(kt[g, :, band], ds_buf[g % 2, band, wide], preferred_element_type=F32)
            x = x * (state[u, "r"] * SCALE)
            first_head = lax.broadcasted_iota(jnp.int32, (PAIR, TILE), 0) < HEAD_DIM
            dq[rows, lanes] = jnp.where(first_head, x[:, :TILE], x[:, TILE:]).T.astype(BF16)

        return [emit]

    def key_grads(g, source, weight, acc):
        lanes = slice(g * PAIR, (g + 1) * PAIR)
        both = slice(0, 4 * TILE)

        def scaled():
            state[g, "w"] = jnp.concatenate(
                [
                    (weight[u % WEIGHTS].astype(F32) * state[u, "r"]).astype(BF16)
                    for u in (REACH * g, REACH * g + 1)
                ],
                axis=1,
            )

        def rows_of(rows, wide):
            def emit():
                acc[rows, lanes] = lax.dot_general(
                    source[g % 2, rows, wide],
                    state[g, "w"][:, wide],
                    NT,
                    preferred_element_type=F32,
                )

            return emit

        return [
            scaled,
            rows_of(slice(0, TILE), slice(0, 2 * TILE)),
            rows_of(slice(TILE, BAND * TILE), both),
            rows_of(slice(BAND * TILE, KEYS), slice(2 * TILE, 4 * TILE)),
        ]

    def transposed(g):
        lanes = slice(g * PAIR, (g + 1) * PAIR)

        def one(j):
            def emit():
                rows = slice(j * TILE, (j + 1) * TILE)
                kt[g, :, rows] = k_ext[rows, lanes].T

            return emit

        return [one(j) for j in range(KEY_TILES)]

    count = len(units)
    for step in range(count + 4):
        late = []
        g, odd = divmod(step - 4, 2)
        if 0 <= g < pairs_here:
            late.append(functools.partial(finish, odd == 1, slice(g * PAIR, (g + 1) * PAIR)))
        g, odd = divmod(step - 1, 2)
        if 0 <= g < pairs_here and odd == 0:
            late += transposed(g)
        if 0 <= step - 2 < count:
            late += query_grads(step - 2)
        g, odd = divmod(step - 3, 2)
        if 0 <= g < pairs_here:
            late += key_grads(g, *((ds_buf, qw, dk_acc) if odd else (e_buf, dw, dv_acc)))
        merge(
            scores(step) if step < count else [],
            softmax(step - 1) if 0 <= step - 1 < count else [],
            late,
        )


def scratch(group):
    lanes, band = group * PAIR, BAND * TILE
    return [
        pltpu.VMEM((KEYS, lanes), BF16),
        pltpu.VMEM((KEYS, lanes), BF16),
        pltpu.VMEM((group, PAIR, KEYS), BF16),
        pltpu.VMEM((KEYS, lanes), F32),
        pltpu.VMEM((KEYS, lanes), F32),
        pltpu.VMEM((WEIGHTS, PAIR, 2 * TILE), BF16),
        pltpu.VMEM((WEIGHTS, PAIR, 2 * TILE), BF16),
        pltpu.VMEM((2, band, 2 * TILE), F32),
        pltpu.VMEM((2, band, 2 * TILE), F32),
        pltpu.VMEM((2, KEYS, 4 * TILE), BF16),
        pltpu.VMEM((2, KEYS, 4 * TILE), BF16),
    ]


def edge_kernel(group, chained, place, dead, q, do, k_near, k_mid, v_near, v_mid, halo, *rest):
    rest = rest[chained:]
    dq, part_k, part_v, send, k_ext, v_ext, kt, dk_acc, dv_acc, *bufs = rest
    low_edge = place[0] == 0
    outside = pl.multiple_of(jnp.where(low_edge, 0, 2 * BLOCK), BLOCK)
    inside = pl.multiple_of(jnp.where(low_edge, 2 * BLOCK, 0), BLOCK)

    for row, near, mid, ext in ((0, k_near, k_mid, k_ext), (BLOCK, v_near, v_mid, v_ext)):
        ext[pl.ds(outside, BLOCK)] = halo[row : row + BLOCK]
        ext[BLOCK : 2 * BLOCK] = near[...]
        ext[pl.ds(inside, BLOCK)] = mid[...]

    def finish(keys, lanes):
        acc, part, row, scale = (
            (dk_acc, part_k, 0, SCALE) if keys else (dv_acc, part_v, BLOCK, 1.0)
        )
        send[row : row + BLOCK, lanes] = (acc[pl.ds(outside, BLOCK), lanes] * scale).astype(BF16)
        part[:BLOCK, lanes] = acc[BLOCK : 2 * BLOCK, lanes].astype(BF16)
        part[BLOCK:, lanes] = acc[pl.ds(inside, BLOCK), lanes].astype(BF16)

    base = place[0] * REACH
    attend(group, base, q, do, dq, k_ext, v_ext, kt, dk_acc, dv_acc, dead, bufs, finish)


def inner_kernel(
    group, place, dead, q, do, k, v, chip_k, chip_v, cross_k, cross_v, back, dq_in, *rest
):
    dq, dk, dv, kt, dk_acc, dv_acc, *bufs = rest
    cross = pl.multiple_of(place[0] * BLOCK, BLOCK)
    chip = pl.multiple_of(2 * BLOCK - cross, BLOCK)


    def finish(keys, lanes):
        acc, part, other, row, out, scale = (
            (dk_acc, chip_k, cross_k, 0, dk, SCALE)
            if keys
            else (dv_acc, chip_v, cross_v, BLOCK, dv, 1.0)
        )
        near = acc[pl.ds(cross, BLOCK), lanes] + other[:BLOCK, lanes].astype(F32)
        out[pl.ds(cross, BLOCK), lanes] = (near * scale).astype(BF16)
        middle = acc[BLOCK : 2 * BLOCK, lanes] + part[BLOCK:, lanes].astype(F32)
        middle = middle + other[BLOCK:, lanes].astype(F32)
        out[BLOCK : 2 * BLOCK, lanes] = (middle * scale).astype(BF16)
        far = (acc[pl.ds(chip, BLOCK), lanes] + part[:BLOCK, lanes].astype(F32)) * scale
        far = far + back[row : row + BLOCK, lanes].astype(F32)
        out[pl.ds(chip, BLOCK), lanes] = far.astype(BF16)

    attend(group, REACH, q, do, dq, k, v, kt, dk_acc, dv_acc, dead, bufs, finish)


def pack_kernel(place, k_cross, k_chip, v_cross, v_chip, *outs):
    *cross_out, chip_out = outs
    for row, cross, chip in ((0, k_cross, k_chip), (BLOCK, v_cross, v_chip)):
        chip_out[row : row + BLOCK] = chip[...]
        at = 0
        for out in cross_out:
            out[row : row + BLOCK] = cross[:, at : at + out.shape[1]]
            at += out.shape[1]


def join_kernel(place, dk, dv, back, dk_out, dv_out):
    dk_out[...] = (dk[...].astype(F32) + back[:BLOCK].astype(F32)).astype(BF16)
    dv_out[...] = (dv[...].astype(F32) + back[BLOCK:].astype(F32)).astype(BF16)


def shards(queries, key_states, values, grad_out, tile_pairs, counts):
    rows_dev, width = queries.shape
    tiles_dev = rows_dev // TILE
    n_seq = lax.axis_size("seq")
    me = lax.axis_index("seq")
    chip_swap = [(i, i ^ 1) for i in range(n_seq) if i ^ 1 < n_seq]
    cross_swap = [(i, i + 1) for i in range(1, n_seq - 1, 2)]
    cross_swap = cross_swap + [(b, a) for a, b in cross_swap]
    first = me * tiles_dev
    cross_block = jnp.where(me % 2 == 0, 0, 2)
    cross_place = jnp.reshape(cross_block, (1,)).astype(jnp.int32)
    chip_place = jnp.reshape(2 - cross_block, (1,)).astype(jnp.int32)
    dead = dead_slots(first, tiles_dev, tile_pairs, counts)
    params = pltpu.CompilerParams(vmem_limit_bytes=VMEM_BYTES)
    cost = pl.CostEstimate(flops=1, bytes_accessed=1, transcendentals=0)

    eighth = width // CUTS[-1]
    chunks = [slice(a * eighth, b * eighth) for a, b in zip(CUTS, CUTS[1:])]
    spans = [c.stop - c.start for c in chunks]
    cross_edge = pl.BlockSpec((BLOCK, width), lambda h, place: (place[0], 0))
    chip_edge = pl.BlockSpec((BLOCK, width), lambda h, place: (2 - place[0], 0))
    *cross_out, chip_out = pl.pallas_call(
        pack_kernel,
        grid_spec=pltpu.PrefetchScalarGridSpec(
            num_scalar_prefetch=1,
            grid=(1,),
            in_specs=[cross_edge, chip_edge] * 2,
            out_specs=[pl.BlockSpec((2 * BLOCK, span), lambda h, *_: (0, 0)) for span in spans]
            + [pl.BlockSpec((2 * BLOCK, width), lambda h, *_: (0, 0))],
        ),
        out_shape=[jax.ShapeDtypeStruct((2 * BLOCK, span), BF16) for span in spans]
        + [jax.ShapeDtypeStruct((2 * BLOCK, width), BF16)],
        compiler_params=params,
        cost_estimate=cost,
        name="pack_edges",
    )(cross_place, key_states, key_states, values, values)
    cross_halos = [lax.ppermute(x, "seq", cross_swap) for x in cross_out]
    chip_halo = lax.ppermute(chip_out, "seq", chip_swap)

    def edge(place, halo, column, lanes, earlier):
        group = min(GROUP, lanes // PAIR)
        wide = group * PAIR
        at = column // wide

        def near(h, place, *_):
            return (place[0], at + h)

        def mid(h, *_):
            return (1, at + h)

        def own(h, *_):
            return (0, h)

        one = pl.BlockSpec((BLOCK, wide), near)
        two = pl.BlockSpec((BLOCK, wide), mid)
        double = pl.BlockSpec((2 * BLOCK, wide), own)
        wide_double = pl.BlockSpec((2 * BLOCK, wide), lambda h, *_: (0, at + h))
        operands = [place, dead, queries, grad_out, key_states, key_states]
        operands += [values, values, halo]
        aliases = {}
        for i, array in enumerate(earlier):
            if array is not None:
                aliases[len(operands)] = i
                operands.append(array)
        return pl.pallas_call(
            functools.partial(edge_kernel, group, len(aliases)),
            grid_spec=pltpu.PrefetchScalarGridSpec(
                num_scalar_prefetch=2,
                grid=(lanes // wide,),
                in_specs=[one, one, one, two, one, two, double]
                + [pl.BlockSpec(memory_space=pl.ANY)] * len(aliases),
                out_specs=[one, wide_double, wide_double, double],
                scratch_shapes=scratch(group),
            ),
            out_shape=[
                jax.ShapeDtypeStruct((rows_dev, width), BF16),
                jax.ShapeDtypeStruct((2 * BLOCK, width), BF16),
                jax.ShapeDtypeStruct((2 * BLOCK, width), BF16),
                jax.ShapeDtypeStruct((2 * BLOCK, lanes), BF16),
            ],
            input_output_aliases=aliases,
            compiler_params=params,
            cost_estimate=cost,
            name="edge_tiles",
        )(*operands)

    dq, chip_k, chip_v, chip_send = edge(chip_place, chip_halo, 0, width, [None] * 3)
    chip_back = lax.ppermute(chip_send, "seq", chip_swap)
    cross_k = cross_v = None
    cross_back = []
    for c, halo in zip(chunks, cross_halos):
        dq, cross_k, cross_v, send = edge(
            cross_place, halo, c.start, c.stop - c.start, [dq, cross_k, cross_v]
        )
        cross_back.append(lax.ppermute(send, "seq", cross_swap))

    wide = GROUP * PAIR

    def spec(rows, row):
        return pl.BlockSpec((rows, wide), lambda h, *_: (row, h))

    operands = [cross_place, dead, queries, grad_out, key_states, values]
    operands += [chip_k, chip_v, cross_k, cross_v, chip_back, dq]
    dq, grad_keys, grad_values = pl.pallas_call(
        functools.partial(inner_kernel, GROUP),
        grid_spec=pltpu.PrefetchScalarGridSpec(
            num_scalar_prefetch=2,
            grid=(width // wide,),
            in_specs=[spec(BLOCK, 1)] * 2
            + [spec(KEYS, 0)] * 2
            + [spec(2 * BLOCK, 0)] * 5
            + [pl.BlockSpec(memory_space=pl.ANY)],
            out_specs=[spec(BLOCK, 1), spec(KEYS, 0), spec(KEYS, 0)],
            scratch_shapes=scratch(GROUP)[2:],
        ),
        out_shape=[jax.ShapeDtypeStruct((rows_dev, width), BF16)] * 3,
        input_output_aliases={len(operands) - 1: 0},
        compiler_params=params,
        cost_estimate=cost,
        name="inner_tiles",
    )(*operands)

    for c, span, back in zip(chunks, spans, cross_back):
        at = c.start // span
        edge_spec = pl.BlockSpec((BLOCK, span), lambda h, place, at=at: (place[0], at))
        back_spec = pl.BlockSpec((2 * BLOCK, span), lambda h, *_: (0, 0))
        grad_keys, grad_values = pl.pallas_call(
            join_kernel,
            grid_spec=pltpu.PrefetchScalarGridSpec(
                num_scalar_prefetch=1,
                grid=(1,),
                in_specs=[edge_spec, edge_spec, back_spec],
                out_specs=[edge_spec, edge_spec],
            ),
            out_shape=[jax.ShapeDtypeStruct((rows_dev, width), BF16)] * 2,
            input_output_aliases={1: 0, 2: 1},
            compiler_params=params,
            cost_estimate=cost,
            name="join_edges",
        )(cross_place, grad_keys, grad_values, back)
    return (dq, grad_keys, grad_values)


def solution(mesh):
    rows = P(("grp", "seq"), None)
    return jax.shard_map(
        shards,
        mesh=mesh,
        in_specs=(rows, rows, rows, rows, P("grp", None), P("grp")),
        out_specs=(rows, rows, rows),
        check_vma=False,
    )
```

```python
import functools

import jax
import jax.numpy as jnp
from jax import lax
from jax.experimental import pallas as pl
from jax.experimental.pallas import tpu as pltpu
from jax.sharding import PartitionSpec as P

HEAD_DIM = 64
SCALE = HEAD_DIM ** (-0.5)
SCALE_LOG2 = SCALE * 1.4426950408889634
REACH = 2
BAND = 2 * REACH + 1
TILE = 128
BLOCK = REACH * TILE
PAIR = 2 * HEAD_DIM
DEAD = 1e30
CUTS = (0, 4, 8)
GROUP = 2
WEIGHTS = 6
F32 = jnp.float32
BF16 = jnp.bfloat16
NT = (((1,), (1,)), ((), ()))
VMEM_BYTES = 63 * 1024 * 1024 + 768 * 1024
KEYS = 3 * BLOCK
KEY_TILES = KEYS // TILE


def merge(*sequences):
    items = []
    for place, sequence in enumerate(sequences):
        for at, emit in enumerate(sequence):
            items.append(((at + 0.5) / len(sequence), place, emit))
    items.sort(key=lambda item: item[:2])
    for _, _, emit in items:
        emit()


def by_head(x):
    x = x.T
    first_head = lax.broadcasted_iota(jnp.int32, x.shape, 0) < HEAD_DIM
    zero = jnp.zeros_like(x)
    return jnp.concatenate([jnp.where(first_head, x, zero), jnp.where(first_head, zero, x)], axis=1)


def dead_slots(first, tiles_dev, tile_pairs, counts):
    chosen = lax.dynamic_slice_in_dim(tile_pairs, first, tiles_dev, 0)
    live = lax.dynamic_slice_in_dim(counts, first, tiles_dev, 0)
    own = first + jnp.arange(tiles_dev, dtype=jnp.int32)
    offset = jnp.arange(BAND, dtype=jnp.int32) - REACH
    slot = jnp.arange(tile_pairs.shape[1], dtype=jnp.int32)
    same = chosen[:, None, :] == (own[:, None] + offset[None, :])[:, :, None]
    hit = jnp.any(same & (slot[None, None, :] < live[:, None, None]), axis=2)
    return jnp.where(hit, 0.0, DEAD).astype(F32)


def attend(pairs_here, base, q, do, dq, k_ext, v_ext, kt, dk_acc, dv_acc, dead, bufs, finish):
    qw, dw, s_buf, dp_buf, e_buf, ds_buf = bufs
    units = [(g, n) for g in range(pairs_here) for n in range(REACH)]
    half = 32
    state = {}

    def at(u):
        g, n = units[u]
        lanes = slice(g * PAIR, (g + 1) * PAIR)
        return g, n, lanes, slice(n * TILE, (n + 1) * TILE), slice(n * TILE, (n + BAND) * TILE)

    def scores(u):
        g, n, lanes, rows, band = at(u)
        b, w = u % 2, u % WEIGHTS

        def weights():
            qw[w] = by_head(q[rows, lanes])
            dw[w] = by_head(do[rows, lanes])

        def product():
            state[u, "s"] = jnp.dot(k_ext[band, lanes], qw[w], preferred_element_type=F32)

        def one(o):
            def emit():
                here = slice(o * TILE, (o + 1) * TILE)
                s = state[u, "s"][here]
                s_buf[b, here] = s
                top = jnp.max(s.reshape(TILE // 8, 8, 2 * TILE), axis=0) - dead[base + n, o]
                state[u, "m"] = top if o == 0 else jnp.maximum(state[u, "m"], top)

            return emit

        def grad_probs():
            dp_buf[b] = jnp.dot(v_ext[band, lanes], dw[w], preferred_element_type=F32)

        return [weights, product] + [one(o) for o in range(BAND)] + [grad_probs]

    def softmax(u):
        g, n, lanes, rows, band = at(u)
        b, wide = u % 2, slice(n * 2 * TILE, (n + 1) * 2 * TILE)

        def parts(o):
            return [slice(o * TILE + c, o * TILE + c + half) for c in range(0, TILE, half)]

        def shifted(r):
            return slice(r.start + n * TILE, r.stop + n * TILE)

        def fold(x):
            return jnp.sum(x.reshape(half // 8, 8, 2 * TILE), axis=0)

        def peak():
            state[u, "m"] = jnp.max(state[u, "m"], axis=0, keepdims=True) * SCALE_LOG2
            state[u, "l"] = jnp.zeros((8, 2 * TILE), F32)
            state[u, "d"] = jnp.zeros((8, 2 * TILE), F32)

        def powers(o):
            def emit():
                shift = state[u, "m"] + dead[base + n, o]
                for r in parts(o):
                    e = jnp.exp2(s_buf[b, r] * SCALE_LOG2 - shift)
                    s_buf[b, r] = e
                    e_buf[g % 2, shifted(r), wide] = e.astype(BF16)
                    state[u, "l"] = state[u, "l"] + fold(e)
                    state[u, "d"] = state[u, "d"] + fold(e * dp_buf[b, r])

            return emit

        def total():
            r = 1.0 / jnp.sum(state[u, "l"], axis=0, keepdims=True)
            state[u, "r"] = r
            state[u, "d"] = jnp.sum(state[u, "d"], axis=0, keepdims=True) * r

        def score_grads(o):
            def emit():
                for r in parts(o):
                    ds = s_buf[b, r] * (dp_buf[b, r] - state[u, "d"])
                    ds_buf[g % 2, shifted(r), wide] = ds.astype(BF16)

            return emit

        return (
            [peak]
            + [powers(o) for o in range(BAND)]
            + [total]
            + [score_grads(o) for o in range(BAND)]
        )

    def query_grads(u):
        g, n, lanes, rows, band = at(u)
        wide = slice(n * 2 * TILE, (n + 1) * 2 * TILE)

        def emit():
            x = jnp.dot(kt[g, :, band], ds_buf[g % 2, band, wide], preferred_element_type=F32)
            x = x * (state[u, "r"] * SCALE)
            first_head = lax.broadcasted_iota(jnp.int32, (PAIR, TILE), 0) < HEAD_DIM
            dq[rows, lanes] = jnp.where(first_head, x[:, :TILE], x[:, TILE:]).T.astype(BF16)

        return [emit]

    def key_grads(g, source, weight, acc):
        lanes = slice(g * PAIR, (g + 1) * PAIR)
        both = slice(0, 4 * TILE)

        def scaled():
            state[g, "w"] = jnp.concatenate(
                [
                    (weight[u % WEIGHTS].astype(F32) * state[u, "r"]).astype(BF16)
                    for u in (REACH * g, REACH * g + 1)
                ],
                axis=1,
            )

        def rows_of(rows, wide):
            def emit():
                acc[rows, lanes] = lax.dot_general(
                    source[g % 2, rows, wide],
                    state[g, "w"][:, wide],
                    NT,
                    preferred_element_type=F32,
                )

            return emit

        return [
            scaled,
            rows_of(slice(0, TILE), slice(0, 2 * TILE)),
            rows_of(slice(TILE, BAND * TILE), both),
            rows_of(slice(BAND * TILE, KEYS), slice(2 * TILE, 4 * TILE)),
        ]

    def transposed(g):
        lanes = slice(g * PAIR, (g + 1) * PAIR)

        def one(j):
            def emit():
                rows = slice(j * TILE, (j + 1) * TILE)
                kt[g, :, rows] = k_ext[rows, lanes].T

            return emit

        return [one(j) for j in range(KEY_TILES)]

    count = len(units)
    for step in range(count + 4):
        late = []
        g, odd = divmod(step - 4, 2)
        if 0 <= g < pairs_here:
            late.append(functools.partial(finish, odd == 1, slice(g * PAIR, (g + 1) * PAIR)))
        g, odd = divmod(step - 1, 2)
        if 0 <= g < pairs_here and odd == 0:
            late += transposed(g)
        if 0 <= step - 2 < count:
            late += query_grads(step - 2)
        g, odd = divmod(step - 3, 2)
        if 0 <= g < pairs_here:
            late += key_grads(g, *((ds_buf, qw, dk_acc) if odd else (e_buf, dw, dv_acc)))
        merge(
            scores(step) if step < count else [],
            softmax(step - 1) if 0 <= step - 1 < count else [],
            late,
        )


def scratch(group):
    lanes, band = group * PAIR, BAND * TILE
    return [
        pltpu.VMEM((KEYS, lanes), BF16),
        pltpu.VMEM((KEYS, lanes), BF16),
        pltpu.VMEM((group, PAIR, KEYS), BF16),
        pltpu.VMEM((KEYS, lanes), F32),
        pltpu.VMEM((KEYS, lanes), F32),
        pltpu.VMEM((WEIGHTS, PAIR, 2 * TILE), BF16),
        pltpu.VMEM((WEIGHTS, PAIR, 2 * TILE), BF16),
        pltpu.VMEM((2, band, 2 * TILE), F32),
        pltpu.VMEM((2, band, 2 * TILE), F32),
        pltpu.VMEM((2, KEYS, 4 * TILE), BF16),
        pltpu.VMEM((2, KEYS, 4 * TILE), BF16),
    ]


def edge_kernel(group, chained, place, dead, q, do, k_near, k_mid, v_near, v_mid, halo, *rest):
    rest = rest[chained:]
    dq, part_k, part_v, send, k_ext, v_ext, kt, dk_acc, dv_acc, *bufs = rest
    low_edge = place[0] == 0
    outside = pl.multiple_of(jnp.where(low_edge, 0, 2 * BLOCK), BLOCK)
    inside = pl.multiple_of(jnp.where(low_edge, 2 * BLOCK, 0), BLOCK)

    for row, near, mid, ext in ((0, k_near, k_mid, k_ext), (BLOCK, v_near, v_mid, v_ext)):
        ext[pl.ds(outside, BLOCK)] = halo[row : row + BLOCK]
        ext[BLOCK : 2 * BLOCK] = near[...]
        ext[pl.ds(inside, BLOCK)] = mid[...]

    def finish(keys, lanes):
        acc, part, row, scale = (
            (dk_acc, part_k, 0, SCALE) if keys else (dv_acc, part_v, BLOCK, 1.0)
        )
        send[row : row + BLOCK, lanes] = (acc[pl.ds(outside, BLOCK), lanes] * scale).astype(BF16)
        part[:BLOCK, lanes] = acc[BLOCK : 2 * BLOCK, lanes].astype(BF16)
        part[BLOCK:, lanes] = acc[pl.ds(inside, BLOCK), lanes].astype(BF16)

    base = place[0] * REACH
    attend(group, base, q, do, dq, k_ext, v_ext, kt, dk_acc, dv_acc, dead, bufs, finish)


def inner_kernel(
    group, first_steps, place, dead, q, do, k, v, chip_k, chip_v, cross_k, cross_v, back, early, dq_in, *rest
):
    dq, dk, dv, kt, dk_acc, dv_acc, *bufs = rest
    cross = pl.multiple_of(place[0] * BLOCK, BLOCK)
    chip = pl.multiple_of(2 * BLOCK - cross, BLOCK)


    arrived = jnp.where(pl.program_id(0) < first_steps, 1.0, 0.0)

    def finish(keys, lanes):
        acc, part, other, row, out, scale = (
            (dk_acc, chip_k, cross_k, 0, dk, SCALE)
            if keys
            else (dv_acc, chip_v, cross_v, BLOCK, dv, 1.0)
        )
        near = acc[pl.ds(cross, BLOCK), lanes] + other[:BLOCK, lanes].astype(F32)
        near = near * scale + early[row : row + BLOCK, lanes].astype(F32) * arrived
        out[pl.ds(cross, BLOCK), lanes] = near.astype(BF16)
        middle = acc[BLOCK : 2 * BLOCK, lanes] + part[BLOCK:, lanes].astype(F32)
        middle = middle + other[BLOCK:, lanes].astype(F32)
        out[BLOCK : 2 * BLOCK, lanes] = (middle * scale).astype(BF16)
        far = (acc[pl.ds(chip, BLOCK), lanes] + part[:BLOCK, lanes].astype(F32)) * scale
        far = far + back[row : row + BLOCK, lanes].astype(F32)
        out[pl.ds(chip, BLOCK), lanes] = far.astype(BF16)

    attend(group, REACH, q, do, dq, k, v, kt, dk_acc, dv_acc, dead, bufs, finish)


class Copies:
    def __init__(self, sems):
        self.sems = sems
        self.count = 0
        self.started = {}

    def start(self, piece, source, target):
        copy = pltpu.make_async_copy(source, target, self.sems.at[self.count])
        copy.start()
        self.count += 1
        self.started.setdefault(piece, []).append(copy)

    def wait(self, piece):
        for copy in self.started.pop(piece, []):
            copy.wait()


def pack_kernel(spans, place, keys, values, *rest):
    *cross_out, chip_out, cross_s, chip_s, in_sems, out_sems = rest
    cross = pl.multiple_of(place[0] * BLOCK, BLOCK)
    chip = pl.multiple_of(2 * BLOCK - cross, BLOCK)
    ins, outs = Copies(in_sems), Copies(out_sems)
    for target, at in ((cross_s, cross), (chip_s, chip)):
        for row, source in ((0, keys), (BLOCK, values)):
            ins.start((target is cross_s, row), source.at[pl.ds(at, BLOCK)], target.at[pl.ds(row, BLOCK)])
    for row in (0, BLOCK):
        rows = pl.ds(row, BLOCK)
        ins.wait((True, row))
        at = 0
        for span, out in zip(spans, cross_out):
            outs.start(0, cross_s.at[rows, pl.ds(at, span)], out.at[rows])
            at += span
    for row in (0, BLOCK):
        rows = pl.ds(row, BLOCK)
        ins.wait((False, row))
        outs.start(0, chip_s.at[rows], chip_out.at[rows])
    outs.wait(0)


def join_kernel(place, dk, dv, back, dk_out, dv_out):
    dk_out[...] = (dk[...].astype(F32) + back[:BLOCK].astype(F32)).astype(BF16)
    dv_out[...] = (dv[...].astype(F32) + back[BLOCK:].astype(F32)).astype(BF16)


def shards(queries, key_states, values, grad_out, tile_pairs, counts):
    rows_dev, width = queries.shape
    tiles_dev = rows_dev // TILE
    n_seq = lax.axis_size("seq")
    me = lax.axis_index("seq")
    chip_swap = [(i, i ^ 1) for i in range(n_seq) if i ^ 1 < n_seq]
    cross_swap = [(i, i + 1) for i in range(1, n_seq - 1, 2)]
    cross_swap = cross_swap + [(b, a) for a, b in cross_swap]
    first = me * tiles_dev
    cross_block = jnp.where(me % 2 == 0, 0, 2)
    cross_place = jnp.reshape(cross_block, (1,)).astype(jnp.int32)
    chip_place = jnp.reshape(2 - cross_block, (1,)).astype(jnp.int32)
    dead = dead_slots(first, tiles_dev, tile_pairs, counts)
    params = pltpu.CompilerParams(vmem_limit_bytes=VMEM_BYTES)
    cost = pl.CostEstimate(flops=1, bytes_accessed=1, transcendentals=0)

    eighth = width // CUTS[-1]
    chunks = [slice(a * eighth, b * eighth) for a, b in zip(CUTS, CUTS[1:])]
    spans = [c.stop - c.start for c in chunks]
    wide = GROUP * PAIR
    first_steps = spans[0] // wide
    anywhere = pl.BlockSpec(memory_space=pl.ANY)
    *cross_out, chip_out = pl.pallas_call(
        functools.partial(pack_kernel, spans),
        grid_spec=pltpu.PrefetchScalarGridSpec(
            num_scalar_prefetch=1,
            grid=(1,),
            in_specs=[anywhere] * 2,
            out_specs=[anywhere] * (len(spans) + 1),
            scratch_shapes=[
                pltpu.VMEM((2 * BLOCK, width), BF16),
                pltpu.VMEM((2 * BLOCK, width), BF16),
                pltpu.SemaphoreType.DMA((4,)),
                pltpu.SemaphoreType.DMA((2 * len(spans) + 2,)),
            ],
        ),
        out_shape=[jax.ShapeDtypeStruct((2 * BLOCK, span), BF16) for span in spans]
        + [jax.ShapeDtypeStruct((2 * BLOCK, width), BF16)],
        compiler_params=params,
        cost_estimate=cost,
        name="pack_edges",
    )(cross_place, key_states, values)
    cross_halos = [lax.ppermute(x, "seq", cross_swap) for x in cross_out]
    chip_halo = lax.ppermute(chip_out, "seq", chip_swap)

    def edge(place, halo, column, lanes, earlier):
        group = min(GROUP, lanes // PAIR)
        wide = group * PAIR
        at = column // wide

        def near(h, place, *_):
            return (place[0], at + h)

        def mid(h, *_):
            return (1, at + h)

        def own(h, *_):
            return (0, h)

        one = pl.BlockSpec((BLOCK, wide), near)
        two = pl.BlockSpec((BLOCK, wide), mid)
        double = pl.BlockSpec((2 * BLOCK, wide), own)
        wide_double = pl.BlockSpec((2 * BLOCK, wide), lambda h, *_: (0, at + h))
        operands = [place, dead, queries, grad_out, key_states, key_states]
        operands += [values, values, halo]
        aliases = {}
        for i, array in enumerate(earlier):
            if array is not None:
                aliases[len(operands)] = i
                operands.append(array)
        return pl.pallas_call(
            functools.partial(edge_kernel, group, len(aliases)),
            grid_spec=pltpu.PrefetchScalarGridSpec(
                num_scalar_prefetch=2,
                grid=(lanes // wide,),
                in_specs=[one, one, one, two, one, two, double]
                + [pl.BlockSpec(memory_space=pl.ANY)] * len(aliases),
                out_specs=[one, wide_double, wide_double, double],
                scratch_shapes=scratch(group),
            ),
            out_shape=[
                jax.ShapeDtypeStruct((rows_dev, width), BF16),
                jax.ShapeDtypeStruct((2 * BLOCK, width), BF16),
                jax.ShapeDtypeStruct((2 * BLOCK, width), BF16),
                jax.ShapeDtypeStruct((2 * BLOCK, lanes), BF16),
            ],
            input_output_aliases=aliases,
            compiler_params=params,
            cost_estimate=cost,
            name="edge_tiles",
        )(*operands)

    dq, chip_k, chip_v, chip_send = edge(chip_place, chip_halo, 0, width, [None] * 3)
    chip_back = lax.ppermute(chip_send, "seq", chip_swap)
    cross_k = cross_v = None
    cross_back = []
    for c, halo in zip(chunks, cross_halos):
        dq, cross_k, cross_v, send = edge(
            cross_place, halo, c.start, c.stop - c.start, [dq, cross_k, cross_v]
        )
        cross_back.append(lax.ppermute(send, "seq", cross_swap))

    def spec(rows, row):
        return pl.BlockSpec((rows, wide), lambda h, *_: (row, h))

    operands = [cross_place, dead, queries, grad_out, key_states, values]
    operands += [chip_k, chip_v, cross_k, cross_v, chip_back, cross_back[0], dq]
    def early(h, *_):
        return (0, jnp.minimum(h, first_steps - 1))

    dq, grad_keys, grad_values = pl.pallas_call(
        functools.partial(inner_kernel, GROUP, first_steps),
        grid_spec=pltpu.PrefetchScalarGridSpec(
            num_scalar_prefetch=2,
            grid=(width // wide,),
            in_specs=[spec(BLOCK, 1)] * 2
            + [spec(KEYS, 0)] * 2
            + [spec(2 * BLOCK, 0)] * 5
            + [pl.BlockSpec((2 * BLOCK, wide), early)]
            + [pl.BlockSpec(memory_space=pl.ANY)],
            out_specs=[spec(BLOCK, 1), spec(KEYS, 0), spec(KEYS, 0)],
            scratch_shapes=scratch(GROUP)[2:],
        ),
        out_shape=[jax.ShapeDtypeStruct((rows_dev, width), BF16)] * 3,
        input_output_aliases={len(operands) - 1: 0},
        compiler_params=params,
        cost_estimate=cost,
        name="inner_tiles",
    )(*operands)

    for c, span, back in zip(chunks[1:], spans[1:], cross_back[1:]):
        at = c.start // span
        edge_spec = pl.BlockSpec((BLOCK, span), lambda h, place, at=at: (place[0], at))
        back_spec = pl.BlockSpec((2 * BLOCK, span), lambda h, *_: (0, 0))
        grad_keys, grad_values = pl.pallas_call(
            join_kernel,
            grid_spec=pltpu.PrefetchScalarGridSpec(
                num_scalar_prefetch=1,
                grid=(1,),
                in_specs=[edge_spec, edge_spec, back_spec],
                out_specs=[edge_spec, edge_spec],
            ),
            out_shape=[jax.ShapeDtypeStruct((rows_dev, width), BF16)] * 2,
            input_output_aliases={1: 0, 2: 1},
            compiler_params=params,
            cost_estimate=cost,
            name="join_edges",
        )(cross_place, grad_keys, grad_values, back)
    return (dq, grad_keys, grad_values)


def solution(mesh):
    rows = P(("grp", "seq"), None)
    return jax.shard_map(
        shards,
        mesh=mesh,
        in_specs=(rows, rows, rows, rows, P("grp", None), P("grp")),
        out_specs=(rows, rows, rows),
        check_vma=False,
    )
```

```python
import functools

import jax
import jax.numpy as jnp
from jax import lax
from jax.experimental import pallas as pl
from jax.experimental.pallas import tpu as pltpu
from jax.sharding import PartitionSpec as P

HEAD_DIM = 64
SCALE = HEAD_DIM ** (-0.5)
SCALE_LOG2 = SCALE * 1.4426950408889634
REACH = 2
BAND = 2 * REACH + 1
TILE = 128
BLOCK = REACH * TILE
PAIR = 2 * HEAD_DIM
DEAD = 1e30
CUTS = (0, 4, 8)
GROUP = 2
WEIGHTS = 6
F32 = jnp.float32
BF16 = jnp.bfloat16
NT = (((1,), (1,)), ((), ()))
VMEM_BYTES = 63 * 1024 * 1024 + 768 * 1024
KEYS = 3 * BLOCK
KEY_TILES = KEYS // TILE


def merge(*sequences):
    items = []
    for place, sequence in enumerate(sequences):
        for at, emit in enumerate(sequence):
            items.append(((at + 0.5) / len(sequence), place, emit))
    items.sort(key=lambda item: item[:2])
    for _, _, emit in items:
        emit()


def by_head(x):
    x = x.T
    first_head = lax.broadcasted_iota(jnp.int32, x.shape, 0) < HEAD_DIM
    zero = jnp.zeros_like(x)
    return jnp.concatenate([jnp.where(first_head, x, zero), jnp.where(first_head, zero, x)], axis=1)


def dead_slots(first, tiles_dev, tile_pairs, counts):
    chosen = lax.dynamic_slice_in_dim(tile_pairs, first, tiles_dev, 0)
    live = lax.dynamic_slice_in_dim(counts, first, tiles_dev, 0)
    own = first + jnp.arange(tiles_dev, dtype=jnp.int32)
    offset = jnp.arange(BAND, dtype=jnp.int32) - REACH
    slot = jnp.arange(tile_pairs.shape[1], dtype=jnp.int32)
    same = chosen[:, None, :] == (own[:, None] + offset[None, :])[:, :, None]
    hit = jnp.any(same & (slot[None, None, :] < live[:, None, None]), axis=2)
    return jnp.where(hit, 0.0, DEAD).astype(F32)


def attend(pairs_here, base, q, do, dq, k_ext, v_ext, kt, dk_acc, dv_acc, dead, bufs, finish):
    qw, dw, s_buf, dp_buf, e_buf, ds_buf = bufs
    units = [(g, n) for g in range(pairs_here) for n in range(REACH)]
    half = 32
    state = {}

    def at(u):
        g, n = units[u]
        lanes = slice(g * PAIR, (g + 1) * PAIR)
        return g, n, lanes, slice(n * TILE, (n + 1) * TILE), slice(n * TILE, (n + BAND) * TILE)

    def scores(u):
        g, n, lanes, rows, band = at(u)
        b, w = u % 2, u % WEIGHTS

        def weights():
            qw[w] = by_head(q[rows, lanes])
            dw[w] = by_head(do[rows, lanes])

        def product():
            state[u, "s"] = jnp.dot(k_ext[band, lanes], qw[w], preferred_element_type=F32)

        def one(o):
            def emit():
                here = slice(o * TILE, (o + 1) * TILE)
                s = state[u, "s"][here]
                s_buf[b, here] = s
                top = jnp.max(s.reshape(TILE // 8, 8, 2 * TILE), axis=0) - dead[base + n, o]
                state[u, "m"] = top if o == 0 else jnp.maximum(state[u, "m"], top)

            return emit

        def grad_probs():
            dp_buf[b] = jnp.dot(v_ext[band, lanes], dw[w], preferred_element_type=F32)

        return [weights, product] + [one(o) for o in range(BAND)] + [grad_probs]

    def softmax(u):
        g, n, lanes, rows, band = at(u)
        b, wide = u % 2, slice(n * 2 * TILE, (n + 1) * 2 * TILE)

        def parts(o):
            return [slice(o * TILE + c, o * TILE + c + half) for c in range(0, TILE, half)]

        def shifted(r):
            return slice(r.start + n * TILE, r.stop + n * TILE)

        def fold(x):
            return jnp.sum(x.reshape(half // 8, 8, 2 * TILE), axis=0)

        def peak():
            state[u, "m"] = jnp.max(state[u, "m"], axis=0, keepdims=True) * SCALE_LOG2
            state[u, "l"] = jnp.zeros((8, 2 * TILE), F32)
            state[u, "d"] = jnp.zeros((8, 2 * TILE), F32)

        def powers(o):
            def emit():
                shift = state[u, "m"] + dead[base + n, o]
                for r in parts(o):
                    e = jnp.exp2(s_buf[b, r] * SCALE_LOG2 - shift)
                    s_buf[b, r] = e
                    e_buf[g % 2, shifted(r), wide] = e.astype(BF16)
                    state[u, "l"] = state[u, "l"] + fold(e)
                    state[u, "d"] = state[u, "d"] + fold(e * dp_buf[b, r])

            return emit

        def total():
            r = 1.0 / jnp.sum(state[u, "l"], axis=0, keepdims=True)
            state[u, "r"] = r
            state[u, "d"] = jnp.sum(state[u, "d"], axis=0, keepdims=True) * r

        def score_grads(o):
            def emit():
                for r in parts(o):
                    ds = s_buf[b, r] * (dp_buf[b, r] - state[u, "d"])
                    ds_buf[g % 2, shifted(r), wide] = ds.astype(BF16)

            return emit

        return (
            [peak]
            + [powers(o) for o in range(BAND)]
            + [total]
            + [score_grads(o) for o in range(BAND)]
        )

    def query_grads(u):
        g, n, lanes, rows, band = at(u)
        wide = slice(n * 2 * TILE, (n + 1) * 2 * TILE)

        def emit():
            x = jnp.dot(kt[g, :, band], ds_buf[g % 2, band, wide], preferred_element_type=F32)
            x = x * (state[u, "r"] * SCALE)
            first_head = lax.broadcasted_iota(jnp.int32, (PAIR, TILE), 0) < HEAD_DIM
            dq[rows, lanes] = jnp.where(first_head, x[:, :TILE], x[:, TILE:]).T.astype(BF16)

        return [emit]

    def key_grads(g, source, weight, acc):
        lanes = slice(g * PAIR, (g + 1) * PAIR)
        both = slice(0, 4 * TILE)

        def scaled():
            state[g, "w"] = jnp.concatenate(
                [
                    (weight[u % WEIGHTS].astype(F32) * state[u, "r"]).astype(BF16)
                    for u in (REACH * g, REACH * g + 1)
                ],
                axis=1,
            )

        def rows_of(rows, wide):
            def emit():
                acc[rows, lanes] = lax.dot_general(
                    source[g % 2, rows, wide],
                    state[g, "w"][:, wide],
                    NT,
                    preferred_element_type=F32,
                )

            return emit

        return [
            scaled,
            rows_of(slice(0, TILE), slice(0, 2 * TILE)),
            rows_of(slice(TILE, BAND * TILE), both),
            rows_of(slice(BAND * TILE, KEYS), slice(2 * TILE, 4 * TILE)),
        ]

    def transposed(g):
        lanes = slice(g * PAIR, (g + 1) * PAIR)

        def one(j):
            def emit():
                rows = slice(j * TILE, (j + 1) * TILE)
                kt[g, :, rows] = k_ext[rows, lanes].T

            return emit

        return [one(j) for j in range(KEY_TILES)]

    count = len(units)
    for step in range(count + 4):
        late = []
        g, odd = divmod(step - 4, 2)
        if 0 <= g < pairs_here:
            late.append(functools.partial(finish, odd == 1, slice(g * PAIR, (g + 1) * PAIR)))
        g, odd = divmod(step - 1, 2)
        if 0 <= g < pairs_here and odd == 0:
            late += transposed(g)
        if 0 <= step - 2 < count:
            late += query_grads(step - 2)
        g, odd = divmod(step - 3, 2)
        last = g == pairs_here - 1
        if 0 <= g < pairs_here and not (odd and last):
            late += key_grads(g, *((ds_buf, qw, dk_acc) if odd else (e_buf, dw, dv_acc)))
        if last and not odd:
            late += key_grads(g, ds_buf, qw, dk_acc)
        merge(
            scores(step) if step < count else [],
            softmax(step - 1) if 0 <= step - 1 < count else [],
            late,
        )


def scratch(group):
    lanes, band = group * PAIR, BAND * TILE
    return [
        pltpu.VMEM((KEYS, lanes), BF16),
        pltpu.VMEM((KEYS, lanes), BF16),
        pltpu.VMEM((group, PAIR, KEYS), BF16),
        pltpu.VMEM((KEYS, lanes), F32),
        pltpu.VMEM((KEYS, lanes), F32),
        pltpu.VMEM((WEIGHTS, PAIR, 2 * TILE), BF16),
        pltpu.VMEM((WEIGHTS, PAIR, 2 * TILE), BF16),
        pltpu.VMEM((2, band, 2 * TILE), F32),
        pltpu.VMEM((2, band, 2 * TILE), F32),
        pltpu.VMEM((2, KEYS, 4 * TILE), BF16),
        pltpu.VMEM((2, KEYS, 4 * TILE), BF16),
    ]


def edge_kernel(group, chained, place, dead, q, do, k, v, halo, *rest):
    rest = rest[chained:]
    dq, part, send, k_ext, v_ext, kt, dk_acc, dv_acc, *bufs = rest
    low_edge = place[0] == 0
    outside = pl.multiple_of(jnp.where(low_edge, 0, 2 * BLOCK), BLOCK)
    inside = pl.multiple_of(jnp.where(low_edge, 2 * BLOCK, 0), BLOCK)
    held = pl.multiple_of(jnp.where(low_edge, BLOCK, 0), BLOCK)

    for row, own, ext in ((0, k, k_ext), (BLOCK, v, v_ext)):
        ext[pl.ds(outside, BLOCK)] = halo[row : row + BLOCK]
        ext[pl.ds(held, 2 * BLOCK)] = own[...]

    def finish(keys, lanes):
        acc, row, scale = (dk_acc, 0, SCALE) if keys else (dv_acc, BLOCK, 1.0)
        send[row : row + BLOCK, lanes] = (acc[pl.ds(outside, BLOCK), lanes] * scale).astype(BF16)
        near, mid = slice(2 * row, 2 * row + BLOCK), slice(2 * row + BLOCK, 2 * row + 2 * BLOCK)
        part[near, lanes] = acc[BLOCK : 2 * BLOCK, lanes].astype(BF16)
        part[mid, lanes] = acc[pl.ds(inside, BLOCK), lanes].astype(BF16)

    base = place[0] * REACH
    attend(group, base, q, do, dq, k_ext, v_ext, kt, dk_acc, dv_acc, dead, bufs, finish)


def inner_kernel(
    group, first_steps, place, dead, q, do, k, v, chip_part, cross_part, back, early, dq_in, *rest
):
    dq, dk, dv, kt, dk_acc, dv_acc, *bufs = rest
    cross = pl.multiple_of(place[0] * BLOCK, BLOCK)
    chip = pl.multiple_of(2 * BLOCK - cross, BLOCK)


    arrived = jnp.where(pl.program_id(0) < first_steps, 1.0, 0.0)

    def finish(keys, lanes):
        acc, row, out, scale = (dk_acc, 0, dk, SCALE) if keys else (dv_acc, BLOCK, dv, 1.0)
        rows = pl.ds(2 * row, 2 * BLOCK)
        part, other = chip_part.at[rows], cross_part.at[rows]
        near = acc[pl.ds(cross, BLOCK), lanes] + other[:BLOCK, lanes].astype(F32)
        near = near * scale + early[row : row + BLOCK, lanes].astype(F32) * arrived
        out[pl.ds(cross, BLOCK), lanes] = near.astype(BF16)
        middle = acc[BLOCK : 2 * BLOCK, lanes] + part[BLOCK:, lanes].astype(F32)
        middle = middle + other[BLOCK:, lanes].astype(F32)
        out[BLOCK : 2 * BLOCK, lanes] = (middle * scale).astype(BF16)
        far = (acc[pl.ds(chip, BLOCK), lanes] + part[:BLOCK, lanes].astype(F32)) * scale
        far = far + back[row : row + BLOCK, lanes].astype(F32)
        out[pl.ds(chip, BLOCK), lanes] = far.astype(BF16)

    attend(group, REACH, q, do, dq, k, v, kt, dk_acc, dv_acc, dead, bufs, finish)


class Copies:
    def __init__(self, sems):
        self.sems = sems
        self.count = 0
        self.started = {}

    def start(self, piece, source, target):
        copy = pltpu.make_async_copy(source, target, self.sems.at[self.count])
        copy.start()
        self.count += 1
        self.started.setdefault(piece, []).append(copy)

    def wait(self, piece):
        for copy in self.started.pop(piece, []):
            copy.wait()


def pack_kernel(spans, place, keys, values, *rest):
    *cross_out, chip_out, cross_s, chip_s, in_sems, out_sems = rest
    cross = pl.multiple_of(place[0] * BLOCK, BLOCK)
    chip = pl.multiple_of(2 * BLOCK - cross, BLOCK)
    ins, outs = Copies(in_sems), Copies(out_sems)
    for target, at in ((cross_s, cross), (chip_s, chip)):
        for row, source in ((0, keys), (BLOCK, values)):
            ins.start((target is cross_s, row), source.at[pl.ds(at, BLOCK)], target.at[pl.ds(row, BLOCK)])
    for row in (0, BLOCK):
        rows = pl.ds(row, BLOCK)
        ins.wait((True, row))
        at = 0
        for span, out in zip(spans, cross_out):
            outs.start(0, cross_s.at[rows, pl.ds(at, span)], out.at[rows])
            at += span
    for row in (0, BLOCK):
        rows = pl.ds(row, BLOCK)
        ins.wait((False, row))
        outs.start(0, chip_s.at[rows], chip_out.at[rows])
    outs.wait(0)


def join_kernel(place, dk, dv, back, dk_out, dv_out):
    dk_out[...] = (dk[...].astype(F32) + back[:BLOCK].astype(F32)).astype(BF16)
    dv_out[...] = (dv[...].astype(F32) + back[BLOCK:].astype(F32)).astype(BF16)


def shards(queries, key_states, values, grad_out, tile_pairs, counts):
    rows_dev, width = queries.shape
    tiles_dev = rows_dev // TILE
    n_seq = lax.axis_size("seq")
    me = lax.axis_index("seq")
    chip_swap = [(i, i ^ 1) for i in range(n_seq) if i ^ 1 < n_seq]
    cross_swap = [(i, i + 1) for i in range(1, n_seq - 1, 2)]
    cross_swap = cross_swap + [(b, a) for a, b in cross_swap]
    first = me * tiles_dev
    cross_block = jnp.where(me % 2 == 0, 0, 2)
    cross_place = jnp.reshape(cross_block, (1,)).astype(jnp.int32)
    chip_place = jnp.reshape(2 - cross_block, (1,)).astype(jnp.int32)
    dead = dead_slots(first, tiles_dev, tile_pairs, counts)
    params = pltpu.CompilerParams(vmem_limit_bytes=VMEM_BYTES)
    cost = pl.CostEstimate(flops=1, bytes_accessed=1, transcendentals=0)

    eighth = width // CUTS[-1]
    chunks = [slice(a * eighth, b * eighth) for a, b in zip(CUTS, CUTS[1:])]
    spans = [c.stop - c.start for c in chunks]
    wide = GROUP * PAIR
    first_steps = spans[0] // wide
    anywhere = pl.BlockSpec(memory_space=pl.ANY)
    *cross_out, chip_out = pl.pallas_call(
        functools.partial(pack_kernel, spans),
        grid_spec=pltpu.PrefetchScalarGridSpec(
            num_scalar_prefetch=1,
            grid=(1,),
            in_specs=[anywhere] * 2,
            out_specs=[anywhere] * (len(spans) + 1),
            scratch_shapes=[
                pltpu.VMEM((2 * BLOCK, width), BF16),
                pltpu.VMEM((2 * BLOCK, width), BF16),
                pltpu.SemaphoreType.DMA((4,)),
                pltpu.SemaphoreType.DMA((2 * len(spans) + 2,)),
            ],
        ),
        out_shape=[jax.ShapeDtypeStruct((2 * BLOCK, span), BF16) for span in spans]
        + [jax.ShapeDtypeStruct((2 * BLOCK, width), BF16)],
        compiler_params=params,
        cost_estimate=cost,
        name="pack_edges",
    )(cross_place, key_states, values)
    cross_halos = [lax.ppermute(x, "seq", cross_swap) for x in cross_out]
    chip_halo = lax.ppermute(chip_out, "seq", chip_swap)

    def edge(place, halo, column, lanes, earlier):
        group = 2 * GROUP if earlier[0] is None else GROUP
        wide = group * PAIR
        at = column // wide

        def near(h, place, *_):
            return (place[0], at + h)

        def window(h, place, *_):
            return (place[0] // 2 * BLOCK, (at + h) * wide)

        def own(h, *_):
            return (0, h)

        one = pl.BlockSpec((BLOCK, wide), near)
        two = pl.BlockSpec((pl.Element(2 * BLOCK), pl.Element(wide)), window)
        double = pl.BlockSpec((2 * BLOCK, wide), own)
        wide_part = pl.BlockSpec((4 * BLOCK, wide), lambda h, *_: (0, at + h))
        operands = [place, dead, queries, grad_out, key_states, values, halo]
        aliases = {}
        for i, array in enumerate(earlier):
            if array is not None:
                aliases[len(operands)] = i
                operands.append(array)
        return pl.pallas_call(
            functools.partial(edge_kernel, group, len(aliases)),
            grid_spec=pltpu.PrefetchScalarGridSpec(
                num_scalar_prefetch=2,
                grid=(lanes // wide,),
                in_specs=[one, one, two, two, double]
                + [pl.BlockSpec(memory_space=pl.ANY)] * len(aliases),
                out_specs=[one, wide_part, double],
                scratch_shapes=scratch(group),
            ),
            out_shape=[
                jax.ShapeDtypeStruct((rows_dev, width), BF16),
                jax.ShapeDtypeStruct((4 * BLOCK, width), BF16),
                jax.ShapeDtypeStruct((2 * BLOCK, lanes), BF16),
            ],
            input_output_aliases=aliases,
            compiler_params=params,
            cost_estimate=cost,
            name="edge_tiles",
        )(*operands)

    dq, chip_part, chip_send = edge(chip_place, chip_halo, 0, width, [None] * 2)
    chip_back = lax.ppermute(chip_send, "seq", chip_swap)
    cross_part = None
    cross_back = []
    for c, halo in zip(chunks, cross_halos):
        dq, cross_part, send = edge(
            cross_place, halo, c.start, c.stop - c.start, [dq, cross_part]
        )
        cross_back.append(lax.ppermute(send, "seq", cross_swap))

    def spec(rows, row):
        return pl.BlockSpec((rows, wide), lambda h, *_: (row, h))

    operands = [cross_place, dead, queries, grad_out, key_states, values]
    operands += [chip_part, cross_part, chip_back, cross_back[0], dq]
    def early(h, *_):
        return (0, jnp.minimum(h, first_steps - 1))

    dq, grad_keys, grad_values = pl.pallas_call(
        functools.partial(inner_kernel, GROUP, first_steps),
        grid_spec=pltpu.PrefetchScalarGridSpec(
            num_scalar_prefetch=2,
            grid=(width // wide,),
            in_specs=[spec(BLOCK, 1)] * 2
            + [spec(KEYS, 0)] * 2
            + [spec(4 * BLOCK, 0)] * 2
            + [spec(2 * BLOCK, 0)]
            + [pl.BlockSpec((2 * BLOCK, wide), early)]
            + [pl.BlockSpec(memory_space=pl.ANY)],
            out_specs=[spec(BLOCK, 1), spec(KEYS, 0), spec(KEYS, 0)],
            scratch_shapes=scratch(GROUP)[2:],
        ),
        out_shape=[jax.ShapeDtypeStruct((rows_dev, width), BF16)] * 3,
        input_output_aliases={len(operands) - 1: 0},
        compiler_params=params,
        cost_estimate=cost,
        name="inner_tiles",
    )(*operands)

    for c, span, back in zip(chunks[1:], spans[1:], cross_back[1:]):
        at = c.start // span
        edge_spec = pl.BlockSpec((BLOCK, span), lambda h, place, at=at: (place[0], at))
        back_spec = pl.BlockSpec((2 * BLOCK, span), lambda h, *_: (0, 0))
        grad_keys, grad_values = pl.pallas_call(
            join_kernel,
            grid_spec=pltpu.PrefetchScalarGridSpec(
                num_scalar_prefetch=1,
                grid=(1,),
                in_specs=[edge_spec, edge_spec, back_spec],
                out_specs=[edge_spec, edge_spec],
            ),
            out_shape=[jax.ShapeDtypeStruct((rows_dev, width), BF16)] * 2,
            input_output_aliases={1: 0, 2: 1},
            compiler_params=params,
            cost_estimate=cost,
            name="join_edges",
        )(cross_place, grad_keys, grad_values, back)
    return (dq, grad_keys, grad_values)


def solution(mesh):
    rows = P(("grp", "seq"), None)
    return jax.shard_map(
        shards,
        mesh=mesh,
        in_specs=(rows, rows, rows, rows, P("grp", None), P("grp")),
        out_specs=(rows, rows, rows),
        check_vma=False,
    )
```
